128 devices in a mesh: grp: 8 (over x, z_hi), row: 4 (over z_lo, core), col: 4 (over y).
Axes of the slice: x: 4, y: 4, z: 4 (z_hi: 2, z_lo: 2; z = z_hi * 2 + z_lo), core: 2. Of those that a mesh axis runs over, the one named last changes fastest.
Arguments:
- children: float32 [8, 6144, 6144], P('grp', 'row', 'col'), may hold values from -4 to 4
- child_map: int32 [8, 48], replicated, may hold values from 0 to 95, as said below
- panel_inverse: float32 [1024, 1024], P('row'), may hold values from -0.03125 to 0.03125
- pattern: int32 [88, 88], replicated, may hold values 0 or 1
Outputs:
- front: float32 [12288, 12288], P('row', ('grp', 'col'))
- panel_rows: float32 [1024, 12288], P('row', ('grp', 'col'))
The draws below stay inside these ranges and needn't reach their ends.
Inputs may be any that keep to these rules, and one draw needn't show every extreme that they name: Each row of child_map is strictly increasing, and child tile a lies in parent tile block a // 12: child_map[g, a] // 24 == a // 12. In each row of child_map and each block, at most 2 child tiles land in any one run of 3 parent tiles that starts at a multiple of 3, and some run receives exactly 2.
All inputs are finite; a program needn't handle non-finite values.
Results may differ from the reference program's by a relative error of at most 0.000071.
Values sent between devices are 32-bit elements; how exact they have to be, the bound alone decides.
A program may use at most 128 MiB of HBM per device.

```python
import jax
import jax.numpy as jnp
from jax import lax

B = 128
PT = 96
CT = 48
WT = 8
GROUPS = 8
P_SIZE = 12288
C = 6144
W = 1024
PB = 24
CB = 12
SH = 3
CAP = 2
TT = 88
N_GRP = 8
N_ROW = 4
N_COL = 4


def draw_child_map(key, part):
    key = jax.random.fold_in(key, 11)
    key_pos = jax.random.fold_in(key, 1)
    key_pick = jax.random.fold_in(key, 2)
    key_fav = jax.random.fold_in(key, 3)
    pos_scores = jax.random.randint(key_pos, (GROUPS, N_ROW, N_GRP, SH), 0, 1 << 20)
    pos_scores = pos_scores * SH + jnp.arange(SH, dtype=jnp.int32)[None, None, None, :]
    picks = jnp.argsort(pos_scores, axis=3)[:, :, :, :CAP].astype(jnp.int32)
    owners = jnp.arange(N_GRP, dtype=jnp.int32)[None, None, :, None]
    candidates = (owners * SH + picks).reshape(GROUPS, N_ROW, N_GRP * CAP)
    cand_owner = jnp.broadcast_to(owners, (GROUPS, N_ROW, N_GRP, CAP)).reshape(GROUPS, N_ROW, N_GRP * CAP)
    favored = jax.random.randint(key_fav, (GROUPS, N_ROW, 1), 0, N_GRP)
    cand_scores = jax.random.randint(key_pick, (GROUPS, N_ROW, N_GRP * CAP), 0, 1 << 20)
    cand_scores = cand_scores * (N_GRP * CAP) + jnp.arange(N_GRP * CAP, dtype=jnp.int32)[None, None, :]
    cand_scores = cand_scores - jnp.where(cand_owner == favored, 1 << 28, 0).astype(jnp.int32)
    order = jnp.argsort(cand_scores, axis=2)[:, :, :CB]
    chosen = jnp.sort(jnp.take_along_axis(candidates, order, axis=2), axis=2).astype(jnp.int32)
    offsets = (jnp.arange(N_ROW, dtype=jnp.int32) * PB)[None, :, None]
    return (chosen + offsets).reshape(GROUPS, CT).astype(jnp.int32)


def touch_ends(values, stream_key, low, largest):
    longest = values.shape.index(max(values.shape))
    spots = []
    for shift in (0, 1):
        where = [jax.random.randint(jax.random.fold_in(stream_key, axis), (), 0, length) for axis, length in enumerate(values.shape)]
        where[longest] = (where[longest] + shift) % values.shape[longest]
        spots.append(tuple(where))
    return values.at[spots[0]].set(low).at[spots[1]].set(largest)


def steps_of(stream_key, shape, cuts, smallest, top_value):
    gain, own = 1.0, jax.random.fold_in(stream_key, 6)
    for dim, shards_of in cuts:
        draws = jnp.exp(jax.random.uniform(jax.random.fold_in(own, dim), (shards_of,), jnp.float32, smallest / len(cuts), top_value / len(cuts)))
        gain = gain * jnp.repeat(draws, shape[dim] // shards_of).reshape([-1 if axis == dim else 1 for axis in range(len(shape))])
    return gain


def gaussian(key, extent, width, most, cuts=(), kind=jnp.bfloat16):
    drawn = jax.random.normal(key, extent, jnp.float32) * width
    if len(cuts) > 0:
        drawn = steps_of(key, extent, cuts, -0.22, 0.18) * drawn
    return jnp.clip(drawn, min=-most, max=most).astype(kind)


def setup_inputs(seed: int = 0) -> dict:
    splits = jax.random.split(jax.random.key(seed), 5)
    return {
        "children": gaussian(splits[0], (GROUPS, C, C), 0.5, 4.0, ((0, 8), (1, 4), (2, 4)), jnp.float32),
        "child_map": draw_child_map(jax.random.fold_in(splits[4], 71), 0),
        "panel_inverse": gaussian(splits[2], (W, W), (32 * W) ** -0.5, 0.03125, ((0, 4),), jnp.float32),
        "pattern": touch_ends((jax.random.randint(splits[3], (TT, TT), 0, 3) < 2).astype(jnp.int32), jax.random.fold_in(splits[3], 1), 0, 1),
    }


def stored(matrix):
    return matrix.reshape(matrix.shape[0], N_COL, N_GRP, SH * B).transpose(0, 2, 1, 3).reshape(matrix.shape[0], P_SIZE)


def reference(children, child_map, panel_inverse, pattern):
    blocks = jnp.zeros((PT, PT, B, B), jnp.float32)
    for member in range(GROUPS):
        tiles = children[member].reshape(CT, B, CT, B).transpose(0, 2, 1, 3)
        places = child_map[member]
        blocks = blocks.at[places[:, None], places[None, :]].add(tiles)
    assembled = blocks.transpose(0, 2, 1, 3).reshape(P_SIZE, P_SIZE)
    factor_rows = jnp.dot(panel_inverse, assembled[:W], precision=lax.Precision.HIGHEST)
    tile_mask = jnp.zeros((PT, PT), jnp.float32).at[WT:, WT:].set(pattern.astype(jnp.float32))
    weights = jnp.broadcast_to(tile_mask[:, None, :, None], (PT, B, PT, B)).reshape(P_SIZE, P_SIZE)
    product = jnp.dot(factor_rows.T, factor_rows, precision=lax.Precision.HIGHEST)
    updated = assembled - weights * product
    return stored(updated), stored(factor_rows)
```

```python
import functools

import jax
import jax.numpy as jnp
from jax import lax
from jax.experimental import pallas as pl
from jax.experimental.pallas import tpu as pltpu
from jax.sharding import PartitionSpec as P

MESH = pl.DeviceIdType.MESH
B = 128
GROUPS = 8
PB = 24
CB = 12
SH = 3
WT = 8
W = 1024
NX = 4
NY = 4
HALF = 6
HROWS = HALF * B
SLOTS = 2 * HROWS
TILES = 2 * HALF
ZERO = NX * 2 * HALF
NONE = 1000
WIDTH = SH * B
BIG = 3072


def pack_kernel(map_ref, child_ref, pack_ref, rows_ref, cols_ref, held, in_sems, sems):
    g = lax.axis_index("grp")
    r = lax.axis_index("row")
    c = lax.axis_index("col")
    x, zh = g // 2, lax.rem(g, 2)
    loads = []
    for n in range(4):
        span = pl.ds(n * HROWS // 2, HROWS // 2)
        loads.append(pltpu.make_async_copy(child_ref.at[span, :], held.at[span, :], in_sems.at[n]))
        loads[n].start()

    @pl.loop(0, 2 * NX * PB)
    def _(i):
        rows_ref[i] = jnp.int32(NONE)

    for i in range(2 * NX * 4):
        cols_ref[i] = jnp.int32(NONE)

    @pl.loop(0, NX)
    def _(s):
        child = 2 * s + zh
        for a in range(CB):
            i = map_ref[child, r * CB + a] - r * PB
            rows_ref[(a // HALF) * NX * PB + s * PB + i] = jnp.int32(a % HALF)
        for d in range(2):
            mine = 2 * x + (zh if d == 0 else 1 - zh)
            before = jnp.int32(-1)
            for q in range(CB):
                p = map_ref[child, c * CB + q] - c * PB
                owner = p // SH
                slot = jnp.where(owner == before, 1, 0)
                before = owner
                j = jnp.where(owner == mine, p - owner * SH, 3)
                cols_ref[d * NX * 4 + s * 4 + j] = (s * 2 + slot) * HALF

    owners, slots = [], []
    for q in range(CB):
        owners.append((map_ref[g, c * CB + q] - c * PB) // SH)
        slots.append(jnp.where(owners[q] == owners[q - 1], 1, 0) if q else jnp.int32(0))
    copies = []
    for h in range(2):
        loads[2 * h].wait()
        loads[2 * h + 1].wait()
        for q in range(CB):
            copy = pltpu.make_async_copy(
                held.at[pl.ds(h * HROWS, HROWS), pl.ds(q * B, B)],
                pack_ref.at[h, owners[q], pl.ds(pl.multiple_of(slots[q] * HROWS, HROWS), HROWS), :],
                sems.at[h, q],
            )
            copy.start()
            copies.append(copy)
    for copy in copies:
        copy.wait()


def front_kernel(
    rows_ref, cols_ref, pattern_ref, pack_ref, inverse_ref,
    front_ref, panel_ref,
    as_ref, ao_ref, bs_ref, bo_ref,
    out_part, in_part, product, product_out,
    own, own_hi, own_lo, near, far,
    inverse_all, top_hi, top_lo,
    x_send, x_recv, x_local, z_send, z_recv, i_send, i_recv, i_local,
    r_send, r_recv, y_send, y_recv, n_send, n_recv, n_local, f_send, f_recv,
    p_send, p_recv, go,
):
    g = lax.axis_index("grp")
    r = lax.axis_index("row")
    c = lax.axis_index("col")
    x, zh = g // 2, lax.rem(g, 2)

    def at(grp=None, row=None, col=None):
        return {
            "grp": g if grp is None else grp,
            "row": r if row is None else row,
            "col": c if col is None else col,
        }

    def x_peer(d):
        return at(grp=lax.rem(x + d, NX) * 2 + zh)

    def y_peer(d):
        return at(col=lax.rem(c + d, NY))

    z_peer = at(grp=2 * x + 1 - zh)

    barrier = pltpu.get_barrier_semaphore()
    peers = [x_peer(d) for d in range(1, NX)] + [y_peer(d) for d in range(1, NY)]
    peers += [at(row=lax.rem(r + d, 4)) for d in range(1, 4)] + [z_peer]
    for peer in peers:
        pl.semaphore_signal(barrier, inc=1, device_id=peer, device_id_type=MESH)
    pl.semaphore_wait(barrier, len(peers))

    def remote(src, dst, send, recv, device):
        return pltpu.make_async_remote_copy(
            src_ref=src, dst_ref=dst, send_sem=send, recv_sem=recv,
            device_id=device, device_id_type=MESH,
        )

    chunks = [as_ref, ao_ref, bs_ref, bo_ref]

    def x_copy(k, d):
        owner = lax.rem(x + d, NX) * 2 + (zh if k % 2 == 0 else 1 - zh)
        return remote(
            pack_ref.at[k // 2, owner],
            chunks[k].at[pl.ds(x * TILES, TILES)],
            x_send.at[k * 3 + d - 1], x_recv.at[k * 3 + d - 1], x_peer(d),
        )

    def x_arrival(k, d):
        source = lax.rem(x + NX - d, NX)
        return remote(
            pack_ref.at[k // 2, 0],
            chunks[k].at[pl.ds(source * TILES, TILES)],
            x_send.at[k * 3 + d - 1], x_recv.at[k * 3 + d - 1], x_peer(NX - d),
        )

    def x_own(k):
        owner = 2 * x + (zh if k % 2 == 0 else 1 - zh)
        return pltpu.make_async_copy(
            pack_ref.at[k // 2, owner],
            chunks[k].at[pl.ds(x * TILES, TILES)],
            x_local.at[k],
        )

    def x_start(k):
        for d in (2, 1, 3):
            x_copy(k, d).start()
        x_own(k).start()

    def x_wait(k):
        x_own(k).wait()
        for d in range(1, NX):
            x_arrival(k, d).wait_recv()

    def inverse_copy():
        return remote(
            inverse_ref,
            inverse_all.at[pl.ds(pl.multiple_of(r * 256, 256), 256), :],
            i_send, i_recv.at[r - 1], at(row=0),
        )

    for ref in chunks:
        ref[ZERO] = jnp.zeros((B, B), jnp.float32)

    @pl.when(r == 0)
    def _():
        x_start(1)
        x_start(0)
        pltpu.make_async_copy(inverse_ref, inverse_all.at[pl.ds(0, 256), :], i_local).start()

    @pl.when(r > 0)
    def _():
        inverse_copy().start()

    @pl.when(r > 1)
    def _():
        x_start(1)
        x_start(3)
        x_start(0)
        x_start(2)

    def tile(d, i, j, use):
        total = None
        for s in range(NX):
            for h, ref in use:
                index = jnp.minimum(
                    rows_ref[h * NX * PB + s * PB + i] + cols_ref[d * NX * 4 + s * 4 + j], ZERO
                )
                value = ref[index]
                total = value if total is None else total + value
        return total

    def spread(first, last, d, put):
        a_ref, b_ref = (as_ref, bs_ref) if d == 0 else (ao_ref, bo_ref)
        for low, high, use in (
            (0, 9, ((0, a_ref),)),
            (9, 15, ((0, a_ref), (1, b_ref))),
            (15, 24, ((1, b_ref),)),
        ):
            low, high = max(low, first), min(high, last)
            if low < high:

                @pl.loop(low, high)
                def _(i):
                    for j in range(SH):
                        put(i, j, tile(d, i, j, use))

    def rows_of(i):
        return pl.ds(pl.multiple_of(i * B, B), B)

    def put_out(i, j, value):
        out_part[rows_of(i), j * B : (j + 1) * B] = value

    def z_copy(part):
        span = pl.ds(0, W) if part == 0 else pl.ds(W, BIG - W)
        return remote(
            out_part.at[span, :], in_part.at[span, :],
            z_send.at[part], z_recv.at[part], z_peer,
        )

    def own_tile(ref, col, j):
        return ref.at[pl.ds(pl.multiple_of(col * WIDTH + j * B, B), B), :]

    def r_copy(j, d):
        return remote(
            own_tile(own, c, j), own_tile(own, c, j),
            r_send.at[(d - 1) * 3 + j], r_recv.at[j], at(row=r + d),
        )

    def y_copy(j, d):
        return remote(
            own_tile(own, c, j), own_tile(own, c, j),
            y_send.at[(d - 1) * 3 + j], y_recv.at[(d - 1) * 3 + j], y_peer(d),
        )

    def y_arrival(j, d):
        source = lax.rem(c + NY - d, NY)
        return remote(
            own_tile(own, source, j), own_tile(own, source, j),
            y_send.at[(d - 1) * 3 + j], y_recv.at[(d - 1) * 3 + j], y_peer(NY - d),
        )

    @pl.when(r == 0)
    def _():
        x_wait(1)
        spread(0, WT, 1, put_out)
        z_copy(0).start()
        x_wait(0)
        pl.semaphore_signal(go, inc=1, device_id=at(row=1), device_id_type=MESH)
        x_start(3)
        x_start(2)

        def put_top(i, j, value):
            product[rows_of(i), j * B : (j + 1) * B] = value

        spread(0, WT, 0, put_top)
        for k in range(1, 4):
            remote(
                inverse_ref, inverse_all.at[pl.ds(k * 256, 256), :],
                i_send, i_recv.at[k - 1], at(row=k),
            ).wait_recv()
        pltpu.make_async_copy(inverse_ref, inverse_all.at[pl.ds(0, 256), :], i_local).wait()
        z_copy(0).wait_recv()

        @pl.loop(0, WT)
        def _(i):
            value = product[rows_of(i), :] + in_part[rows_of(i), :]
            high = value.astype(jnp.bfloat16)
            top_hi[rows_of(i), :] = high
            top_lo[rows_of(i), :] = (value - high.astype(jnp.float32)).astype(jnp.bfloat16)

        for k in range(4):
            block = inverse_all[k * 256 : (k + 1) * 256, :]
            high = block.astype(jnp.bfloat16)
            low = (block - high.astype(jnp.float32)).astype(jnp.bfloat16)
            dot = functools.partial(jnp.dot, preferred_element_type=jnp.float32)
            part = dot(high, top_lo[...]) + dot(low, top_hi[...]) + dot(high, top_hi[...])
            own[pl.ds(pl.multiple_of(c * WIDTH, WIDTH), WIDTH), k * 256 : (k + 1) * 256] = part.T
        for j in range(SH):
            r_copy(j, 1).start()
            r_copy(j, 2).start()
            for d in range(1, NY):
                y_copy(j, d).start()

    @pl.when(r == 1)
    def _():
        pl.semaphore_wait(go, 1)
        x_start(1)
        x_start(3)
        x_start(0)
        x_start(2)

    @pl.when(r > 1)
    def _():
        x_wait(1)
        spread(0, WT, 1, put_out)
        z_copy(0).start()

    @pl.when(r > 0)
    def _():
        for j in range(SH):
            remote(
                own_tile(own, c, j), own_tile(own, c, j),
                r_send.at[j], r_recv.at[j], at(row=r - 1),
            ).wait_recv()

            @pl.when(r == 2)
            def _():
                r_copy(j, 1).start()

            for d in range(1, NY):
                y_copy(j, d).start()

    @pl.when(r == 1)
    def _():
        x_wait(1)
        spread(0, WT, 1, put_out)
        z_copy(0).start()

    x_wait(3)
    spread(WT, PB, 1, put_out)
    z_copy(1).start()

    panel_ref[...] = own[
        pl.ds(pl.multiple_of(c * WIDTH, WIDTH), WIDTH), pl.ds(pl.multiple_of(r * 256, 256), 256)
    ].T

    def n_copy(j):
        return remote(
            own_tile(own, r, j), near.at[pl.ds(j * B, B), :],
            n_send.at[j], n_recv.at[j], at(grp=lax.rem(x + NX - c, NX) * 2 + zh),
        )

    def n_arrival(j):
        return remote(
            own_tile(own, r, j), near.at[pl.ds(j * B, B), :],
            n_send.at[j], n_recv.at[j], at(grp=lax.rem(x + c, NX) * 2 + zh),
        )

    def n_own(j):
        return pltpu.make_async_copy(own_tile(own, r, j), near.at[pl.ds(j * B, B), :], n_local.at[j])

    def f_copy(j):
        return remote(
            near.at[pl.ds(j * B, B), :], far.at[pl.ds(j * B, B), :],
            f_send.at[j], f_recv.at[j], z_peer,
        )

    for j in range(SH):
        for d in range(1, NY):

            @pl.when(lax.rem(c + NY - r, NY) == d)
            def _():
                y_arrival(j, d).wait_recv()

        @pl.when(c > 0)
        def _():
            n_copy(j).start()

        @pl.when(c == 0)
        def _():
            n_own(j).start()

    for j in range(SH):

        @pl.when(c > 0)
        def _():
            n_arrival(j).wait_recv()

        @pl.when(c == 0)
        def _():
            n_own(j).wait()

        f_copy(j).start()

    for j in range(SH):
        for d in range(1, NY):

            @pl.when(lax.rem(c + NY - r, NY) != d)
            def _():
                y_arrival(j, d).wait_recv()

    @pl.loop(0, NY * SH)
    def _(t):
        value = own[rows_of(t), :]
        high = value.astype(jnp.bfloat16)
        own_hi[rows_of(t), :] = high
        own_lo[rows_of(t), :] = (value - high.astype(jnp.float32)).astype(jnp.bfloat16)

    def place(b, j):
        return 3 * (2 * lax.rem(x + c, NX) + (zh if b == 0 else 1 - zh)) + j

    def p_copy(b, j, d):
        n = (b * 3 + j) * 3 + d - 1
        return remote(
            product_out.at[pl.ds(n * B, B), :], product.at[rows_of(place(b, j)), :],
            p_send.at[n], p_recv.at[n], y_peer(d),
        )

    def p_arrival(b, j, d):
        n = (b * 3 + j) * 3 + d - 1
        source = lax.rem(c + NY - d, NY)
        index = 3 * (2 * lax.rem(x + source, NX) + (zh if b == 0 else 1 - zh)) + j
        return remote(
            product_out.at[pl.ds(n * B, B), :], product.at[rows_of(index), :],
            p_send.at[n], p_recv.at[n], y_peer(NY - d),
        )

    def times(a, b):
        return lax.dot_general(a, b, (((1,), (1,)), ((), ())), preferred_element_type=jnp.float32)

    for b in range(2):
        for j in range(SH):
            if b == 1:
                f_copy(j).wait_recv()
            value = (near, far)[b][j * B : (j + 1) * B, :]
            high = value.astype(jnp.bfloat16)
            low = (value - high.astype(jnp.float32)).astype(jnp.bfloat16)
            for d in (2, 1, 3, 0):
                col = lax.rem(c + d, NY)
                span = pl.ds(pl.multiple_of(col * WIDTH, WIDTH), WIDTH)
                got = (
                    times(high, own_lo[span, :]) + times(low, own_hi[span, :])
                    + times(high, own_hi[span, :])
                )
                if d == 0:
                    product[rows_of(place(b, j)), :] = got
                else:
                    n = (b * 3 + j) * 3 + d - 1
                    product_out[n * B : (n + 1) * B, :] = got
                    p_copy(b, j, d).start()

    @pl.when(r > 0)
    def _():
        x_wait(0)

    x_wait(2)

    @pl.when(r > 0)
    def _():
        z_copy(0).wait_recv()

    z_copy(1).wait_recv()
    for b in range(2):
        for j in range(SH):
            for d in range(1, NY):
                p_arrival(b, j, d).wait_recv()

    def put_front(i, j, value):
        down = r * PB + i - WT
        right = c * PB + g * SH + j - WT
        weight = pattern_ref[jnp.maximum(down, 0), jnp.maximum(right, 0)]
        weight = jnp.where((down >= 0) & (right >= 0), weight, 0).astype(jnp.float32)
        span = (rows_of(i), slice(j * B, (j + 1) * B))
        front_ref[span] = value + in_part[span] - weight * product[span]

    spread(0, PB, 0, put_front)

    for k in range(4):
        for d in range(1, NX):
            x_copy(k, d).wait_send()
    for part in range(2):
        z_copy(part).wait_send()

    @pl.when(r > 0)
    def _():
        inverse_copy().wait_send()

    for j in range(SH):

        @pl.when((r == 0) | (r == 2))
        def _():
            r_copy(j, 1).wait_send()

        @pl.when(r == 0)
        def _():
            r_copy(j, 2).wait_send()

        for d in range(1, NY):
            y_copy(j, d).wait_send()

        @pl.when(c > 0)
        def _():
            n_copy(j).wait_send()

        f_copy(j).wait_send()
        for b in range(2):
            for d in range(1, NY):
                p_copy(b, j, d).wait_send()


def per_device(children, child_map, panel_inverse, pattern):
    anywhere = pl.BlockSpec(memory_space=pl.ANY)
    smem = pl.BlockSpec(memory_space=pltpu.SMEM)
    vmem = pl.BlockSpec(memory_space=pltpu.VMEM)
    pack, rows, cols = pl.pallas_call(
        pack_kernel,
        name="pack",
        out_shape=(
            jax.ShapeDtypeStruct((2, GROUPS, SLOTS, B), jnp.float32),
            jax.ShapeDtypeStruct((2 * NX * PB,), jnp.int32),
            jax.ShapeDtypeStruct((2 * NX * 4,), jnp.int32),
        ),
        in_specs=[smem, anywhere],
        out_specs=(anywhere, smem, smem),
        scratch_shapes=[
            pltpu.VMEM((CB * B, CB * B), jnp.float32),
            pltpu.SemaphoreType.DMA((4,)),
            pltpu.SemaphoreType.DMA((2, CB)),
        ],
        compiler_params=pltpu.CompilerParams(vmem_limit_bytes=16 * 2**20),
    )(child_map, children[0])
    pack = pack.reshape(2, GROUPS, TILES, B, B)
    f32, bf16 = jnp.float32, jnp.bfloat16
    dma = pltpu.SemaphoreType.DMA
    chunk = pltpu.VMEM((ZERO + 1, B, B), f32)
    return pl.pallas_call(
        front_kernel,
        name="front",
        out_shape=(
            jax.ShapeDtypeStruct((BIG, WIDTH), f32),
            jax.ShapeDtypeStruct((256, WIDTH), f32),
        ),
        in_specs=[smem, smem, smem, anywhere, anywhere],
        out_specs=(vmem, vmem),
        scratch_shapes=[
            chunk, chunk, chunk, chunk,
            pltpu.VMEM((BIG, WIDTH), f32), pltpu.VMEM((BIG, WIDTH), f32),
            pltpu.VMEM((BIG, WIDTH), f32), pltpu.VMEM((18 * B, WIDTH), f32),
            pltpu.VMEM((NY * WIDTH, W), f32),
            pltpu.VMEM((NY * WIDTH, W), bf16), pltpu.VMEM((NY * WIDTH, W), bf16),
            pltpu.VMEM((WIDTH, W), f32), pltpu.VMEM((WIDTH, W), f32),
            pltpu.VMEM((W, W), f32),
            pltpu.VMEM((W, WIDTH), bf16), pltpu.VMEM((W, WIDTH), bf16),
            dma((12,)), dma((12,)), dma((4,)), dma((2,)), dma((2,)), dma(()), dma((3,)), dma(()),
            dma((6,)), dma((3,)), dma((9,)), dma((9,)), dma((3,)), dma((3,)), dma((3,)), dma((3,)), dma((3,)),
            dma((18,)), dma((18,)), pltpu.SemaphoreType.REGULAR,
        ],
        compiler_params=pltpu.CompilerParams(
            collective_id=1, has_side_effects=True, vmem_limit_bytes=62 * 2**20
        ),
    )(rows, cols, pattern, pack, panel_inverse)


def solution(mesh):
    placed = (P("grp", "row", "col"), P(), P("row", None), P())
    return jax.shard_map(
        per_device,
        mesh=mesh,
        in_specs=placed,
        out_specs=(P("row", ("grp", "col")), P("row", ("grp", "col"))),
        check_vma=False,
    )
```

```python
import functools

import jax
import jax.numpy as jnp
from jax import lax
from jax.experimental import pallas as pl
from jax.experimental.pallas import tpu as pltpu
from jax.sharding import PartitionSpec as P

MESH = pl.DeviceIdType.MESH
B = 128
GROUPS = 8
PB = 24
CB = 12
SH = 3
WT = 8
W = 1024
NX = 4
NY = 4
HALF = 6
HROWS = HALF * B
SLOTS = 2 * HROWS
TILES = 2 * HALF
ZERO = NX * 2 * HALF
NONE = 1000
WIDTH = SH * B
BIG = 3072


def pack_kernel(map_ref, child_ref, pack_ref, rows_ref, cols_ref, held, in_sems, sems):
    g = lax.axis_index("grp")
    r = lax.axis_index("row")
    c = lax.axis_index("col")
    x, zh = g // 2, lax.rem(g, 2)
    loads = []
    for n in range(4):
        span = pl.ds(n * HROWS // 2, HROWS // 2)
        loads.append(pltpu.make_async_copy(child_ref.at[span, :], held.at[span, :], in_sems.at[n]))
        loads[n].start()

    @pl.loop(0, 2 * NX * PB)
    def _(i):
        rows_ref[i] = jnp.int32(NONE)

    for i in range(2 * NX * 4):
        cols_ref[i] = jnp.int32(NONE)

    @pl.loop(0, NX)
    def _(s):
        child = 2 * s + zh
        for a in range(CB):
            i = map_ref[child, r * CB + a] - r * PB
            rows_ref[(a // HALF) * NX * PB + s * PB + i] = jnp.int32(a % HALF)
        for d in range(2):
            mine = 2 * x + (zh if d == 0 else 1 - zh)
            before = jnp.int32(-1)
            for q in range(CB):
                p = map_ref[child, c * CB + q] - c * PB
                owner = p // SH
                slot = jnp.where(owner == before, 1, 0)
                before = owner
                j = jnp.where(owner == mine, p - owner * SH, 3)
                cols_ref[d * NX * 4 + s * 4 + j] = (s * 2 + slot) * HALF

    owners, slots = [], []
    for q in range(CB):
        owners.append((map_ref[g, c * CB + q] - c * PB) // SH)
        slots.append(jnp.where(owners[q] == owners[q - 1], 1, 0) if q else jnp.int32(0))
    copies = []
    for h in range(2):
        loads[2 * h].wait()
        loads[2 * h + 1].wait()
        for q in range(CB):
            copy = pltpu.make_async_copy(
                held.at[pl.ds(h * HROWS, HROWS), pl.ds(q * B, B)],
                pack_ref.at[h, owners[q], pl.ds(pl.multiple_of(slots[q] * HROWS, HROWS), HROWS), :],
                sems.at[h, q],
            )
            copy.start()
            copies.append(copy)
    for copy in copies:
        copy.wait()


def front_kernel(
    rows_ref, cols_ref, pattern_ref, pack_ref, inverse_ref,
    front_ref, panel_ref,
    as_ref, ao_ref, bs_ref, bo_ref,
    out_part, in_part, product, product_out,
    own, own_hi, own_lo, near, far,
    inverse_all, top_hi, top_lo,
    x_send, x_recv, x_local, z_send, z_recv, i_send, i_recv, i_local,
    r_send, r_recv, c_send, c_recv, y_send, y_recv, n_send, n_recv, n_local, f_send, f_recv,
    p_send, p_recv, go,
):
    g = lax.axis_index("grp")
    r = lax.axis_index("row")
    c = lax.axis_index("col")
    x, zh = g // 2, lax.rem(g, 2)

    def at(grp=None, row=None, col=None):
        return {
            "grp": g if grp is None else grp,
            "row": r if row is None else row,
            "col": c if col is None else col,
        }

    def x_peer(d):
        return at(grp=lax.rem(x + d, NX) * 2 + zh)

    def y_peer(d):
        return at(col=lax.rem(c + d, NY))

    z_peer = at(grp=2 * x + 1 - zh)
    core = lax.rem(r, 2)
    other_core = at(row=r + 1 - 2 * core)

    barrier = pltpu.get_barrier_semaphore()
    peers = [x_peer(d) for d in range(1, NX)] + [y_peer(d) for d in range(1, NY)]
    peers += [at(row=lax.rem(r + d, 4)) for d in range(1, 4)] + [z_peer]
    for peer in peers:
        pl.semaphore_signal(barrier, inc=1, device_id=peer, device_id_type=MESH)
    pl.semaphore_wait(barrier, len(peers))

    def remote(src, dst, send, recv, device):
        return pltpu.make_async_remote_copy(
            src_ref=src, dst_ref=dst, send_sem=send, recv_sem=recv,
            device_id=device, device_id_type=MESH,
        )

    chunks = [as_ref, ao_ref, bs_ref, bo_ref]

    def x_copy(k, d):
        owner = lax.rem(x + d, NX) * 2 + (zh if k % 2 == 0 else 1 - zh)
        return remote(
            pack_ref.at[k // 2, owner],
            chunks[k].at[pl.ds(x * TILES, TILES)],
            x_send.at[k * 3 + d - 1], x_recv.at[k * 3 + d - 1], x_peer(d),
        )

    def x_arrival(k, d):
        source = lax.rem(x + NX - d, NX)
        return remote(
            pack_ref.at[k // 2, 0],
            chunks[k].at[pl.ds(source * TILES, TILES)],
            x_send.at[k * 3 + d - 1], x_recv.at[k * 3 + d - 1], x_peer(NX - d),
        )

    def x_own(k):
        owner = 2 * x + (zh if k % 2 == 0 else 1 - zh)
        return pltpu.make_async_copy(
            pack_ref.at[k // 2, owner],
            chunks[k].at[pl.ds(x * TILES, TILES)],
            x_local.at[k],
        )

    def x_start(k):
        for d in (2, 1, 3):
            x_copy(k, d).start()
        x_own(k).start()

    def x_wait(k):
        x_own(k).wait()
        for d in range(1, NX):
            x_arrival(k, d).wait_recv()

    def inverse_copy():
        return remote(
            inverse_ref,
            inverse_all.at[pl.ds(pl.multiple_of(r * 256, 256), 256), :],
            i_send, i_recv.at[r - 1], at(row=0),
        )

    for ref in chunks:
        ref[ZERO] = jnp.zeros((B, B), jnp.float32)

    @pl.when(r == 0)
    def _():
        x_start(1)
        x_start(0)
        pltpu.make_async_copy(inverse_ref, inverse_all.at[pl.ds(0, 256), :], i_local).start()

    @pl.when(r > 0)
    def _():
        inverse_copy().start()

    @pl.when(r > 1)
    def _():
        x_start(1)
        x_start(3)

    def tile(d, i, j, use):
        total = None
        for s in range(NX):
            for h, ref in use:
                index = jnp.minimum(
                    rows_ref[h * NX * PB + s * PB + i] + cols_ref[d * NX * 4 + s * 4 + j], ZERO
                )
                value = ref[index]
                total = value if total is None else total + value
        return total

    def spread(first, last, d, put):
        a_ref, b_ref = (as_ref, bs_ref) if d == 0 else (ao_ref, bo_ref)
        for low, high, use in (
            (0, 9, ((0, a_ref),)),
            (9, 15, ((0, a_ref), (1, b_ref))),
            (15, 24, ((1, b_ref),)),
        ):
            low, high = max(low, first), min(high, last)
            if low < high:

                @pl.loop(low, high)
                def _(i):
                    for j in range(SH):
                        put(i, j, tile(d, i, j, use))

    def rows_of(i):
        return pl.ds(pl.multiple_of(i * B, B), B)

    def put_out(i, j, value):
        out_part[rows_of(i), j * B : (j + 1) * B] = value

    def z_copy(part):
        span = pl.ds(part * W, W)
        return remote(
            out_part.at[span, :], in_part.at[span, :],
            z_send.at[part], z_recv.at[part], z_peer,
        )

    def own_tile(ref, col, j):
        return ref.at[pl.ds(pl.multiple_of(col * WIDTH + j * B, B), B), :]

    def own_half(col, j, k):
        start = col * WIDTH + j * B + k * (B // 2)
        return own.at[pl.ds(pl.multiple_of(start, B // 2), B // 2), :]

    def r_copy(j, d):
        part = own_tile(own, c, j) if d == 1 else own_half(c, j, d - 2)
        return remote(part, part, r_send.at[(d - 1) * 3 + j], r_recv.at[j], at(row=d))

    def c_copy(j, d):
        part = own_half(lax.rem(c + NY - d, NY), j, core)
        return remote(part, part, c_send.at[d * 3 + j], c_recv.at[d * 3 + j], other_core)

    def c_arrival(j, d):
        part = own_half(lax.rem(c + NY - d, NY), j, 1 - core)
        return remote(part, part, c_send.at[d * 3 + j], c_recv.at[d * 3 + j], other_core)

    def y_copy(j, d):
        part = own_half(c, j, core)
        n = (d - 1) * 3 + j
        return remote(part, part, y_send.at[n], y_recv.at[n], y_peer(d))

    def y_arrival(j, d):
        part = own_half(lax.rem(c + NY - d, NY), j, core)
        n = (d - 1) * 3 + j
        return remote(part, part, y_send.at[n], y_recv.at[n], y_peer(NY - d))

    @pl.when(r == 0)
    def _():
        x_wait(1)
        spread(0, WT, 1, put_out)
        z_copy(0).start()
        x_wait(0)
        pl.semaphore_signal(go, inc=1, device_id=at(row=1), device_id_type=MESH)
        x_start(3)

        def put_top(i, j, value):
            product[rows_of(i), j * B : (j + 1) * B] = value

        spread(0, WT, 0, put_top)
        for k in range(1, 4):
            remote(
                inverse_ref, inverse_all.at[pl.ds(k * 256, 256), :],
                i_send, i_recv.at[k - 1], at(row=k),
            ).wait_recv()
        pltpu.make_async_copy(inverse_ref, inverse_all.at[pl.ds(0, 256), :], i_local).wait()
        z_copy(0).wait_recv()

        @pl.loop(0, WT)
        def _(i):
            value = product[rows_of(i), :] + in_part[rows_of(i), :]
            high = value.astype(jnp.bfloat16)
            top_hi[rows_of(i), :] = high
            top_lo[rows_of(i), :] = (value - high.astype(jnp.float32)).astype(jnp.bfloat16)

        for k in range(4):
            block = inverse_all[k * 256 : (k + 1) * 256, :]
            high = block.astype(jnp.bfloat16)
            low = (block - high.astype(jnp.float32)).astype(jnp.bfloat16)
            dot = functools.partial(jnp.dot, preferred_element_type=jnp.float32)
            part = dot(high, top_lo[...]) + dot(low, top_hi[...]) + dot(high, top_hi[...])
            own[pl.ds(pl.multiple_of(c * WIDTH, WIDTH), WIDTH), k * 256 : (k + 1) * 256] = part.T
        for j in range(SH):
            r_copy(j, 2).start()
            r_copy(j, 3).start()
            r_copy(j, 1).start()
            for d in range(1, NY):
                y_copy(j, d).start()

    @pl.when(r == 1)
    def _():
        pl.semaphore_wait(go, 1)
        x_start(1)
        x_start(3)

    @pl.when(r > 1)
    def _():
        x_wait(1)
        spread(0, WT, 1, put_out)
        z_copy(0).start()

    @pl.when(r == 1)
    def _():
        for j in range(SH):
            r_copy(j, 1).wait_recv()
            for d in range(1, NY):
                y_copy(j, d).start()

    @pl.when(r > 1)
    def _():
        for j in range(SH):
            part = own_half(c, j, core)
            remote(part, part, r_send.at[j], r_recv.at[j], at(row=0)).wait_recv()
            for d in range(1, NY):
                y_copy(j, d).start()
            c_copy(j, 0).start()

    @pl.when(r == 1)
    def _():
        x_wait(1)
        spread(0, WT, 1, put_out)
        z_copy(0).start()

    x_wait(3)

    @pl.when(r > 0)
    def _():
        x_start(0)

    spread(WT, 2 * WT, 1, put_out)
    z_copy(1).start()


    @pl.when(r > 1)
    def _():
        for j in range(SH):
            c_arrival(j, 0).wait_recv()

    def n_copy(j):
        return remote(
            own_tile(own, r, j), near.at[pl.ds(j * B, B), :],
            n_send.at[j], n_recv.at[j], at(grp=lax.rem(x + 2 * NX - c - j, NX) * 2 + zh),
        )

    def n_arrival(j):
        return remote(
            own_tile(own, r, j), near.at[pl.ds(j * B, B), :],
            n_send.at[j], n_recv.at[j], at(grp=lax.rem(x + c + j, NX) * 2 + zh),
        )

    def n_own(j):
        return pltpu.make_async_copy(own_tile(own, r, j), near.at[pl.ds(j * B, B), :], n_local.at[j])

    def f_copy(j):
        return remote(
            near.at[pl.ds(j * B, B), :], far.at[pl.ds(j * B, B), :],
            f_send.at[j], f_recv.at[j], z_peer,
        )

    for j in range(SH):
        for d in (1, 3, 2):
            y_arrival(j, d).wait_recv()
            c_copy(j, d).start()
        for d in range(1, NY):

            @pl.when(lax.rem(c + NY - r, NY) == d)
            def _():
                c_arrival(j, d).wait_recv()

        @pl.when(lax.rem(c + j, NX) > 0)
        def _():
            n_copy(j).start()

        @pl.when(lax.rem(c + j, NX) == 0)
        def _():
            n_own(j).start()

    x_start(2)

    for j in range(SH):

        @pl.when(lax.rem(c + j, NX) > 0)
        def _():
            n_arrival(j).wait_recv()

        @pl.when(lax.rem(c + j, NX) == 0)
        def _():
            n_own(j).wait()

        f_copy(j).start()

    spread(2 * WT, PB, 1, put_out)
    z_copy(2).start()

    for j in range(SH):
        for d in range(1, NY):

            @pl.when(lax.rem(c + NY - r, NY) != d)
            def _():
                c_arrival(j, d).wait_recv()

    @pl.loop(0, NY * SH)
    def _(t):
        value = own[rows_of(t), :]
        high = value.astype(jnp.bfloat16)
        own_hi[rows_of(t), :] = high
        own_lo[rows_of(t), :] = (value - high.astype(jnp.float32)).astype(jnp.bfloat16)

    def place(b, j):
        return 3 * (2 * lax.rem(x + c + j, NX) + (zh if b == 0 else 1 - zh)) + j

    def p_copy(b, j, d):
        n = (b * 3 + j) * 3 + d - 1
        return remote(
            product_out.at[pl.ds(n * B, B), :], product.at[rows_of(place(b, j)), :],
            p_send.at[n], p_recv.at[n], y_peer(d),
        )

    def p_arrival(b, j, d):
        n = (b * 3 + j) * 3 + d - 1
        source = lax.rem(c + NY - d, NY)
        index = 3 * (2 * lax.rem(x + source + j, NX) + (zh if b == 0 else 1 - zh)) + j
        return remote(
            product_out.at[pl.ds(n * B, B), :], product.at[rows_of(index), :],
            p_send.at[n], p_recv.at[n], y_peer(NY - d),
        )

    def times(a, b):
        return lax.dot_general(a, b, (((1,), (1,)), ((), ())), preferred_element_type=jnp.float32)

    for b in range(2):
        for j in range(SH):
            if b == 1:
                f_copy(j).wait_recv()
            value = (near, far)[b][j * B : (j + 1) * B, :]
            high = value.astype(jnp.bfloat16)
            low = (value - high.astype(jnp.float32)).astype(jnp.bfloat16)
            for d in (2, 1, 3, 0):
                col = lax.rem(c + d, NY)
                span = pl.ds(pl.multiple_of(col * WIDTH, WIDTH), WIDTH)
                got = (
                    times(high, own_lo[span, :]) + times(low, own_hi[span, :])
                    + times(high, own_hi[span, :])
                )
                if d == 0:
                    product[rows_of(place(b, j)), :] = got
                else:
                    n = (b * 3 + j) * 3 + d - 1
                    product_out[n * B : (n + 1) * B, :] = got
                    p_copy(b, j, d).start()

    panel_ref[...] = own[
        pl.ds(pl.multiple_of(c * WIDTH, WIDTH), WIDTH), pl.ds(pl.multiple_of(r * 256, 256), 256)
    ].T

    @pl.when(r > 0)
    def _():
        x_wait(0)

    x_wait(2)

    @pl.when(r > 0)
    def _():
        z_copy(0).wait_recv()

    z_copy(1).wait_recv()
    z_copy(2).wait_recv()

    def put_front(i, j, value):
        span = (rows_of(i), slice(j * B, (j + 1) * B))
        front_ref[span] = value + in_part[span]

    spread(0, PB, 0, put_front)

    for b in range(2):
        for j in range(SH):
            for d in range(1, NY):
                p_arrival(b, j, d).wait_recv()

    @pl.loop(0, PB)
    def _(i):
        for j in range(SH):
            down = r * PB + i - WT
            right = c * PB + g * SH + j - WT
            weight = pattern_ref[jnp.maximum(down, 0), jnp.maximum(right, 0)]
            weight = jnp.where((down >= 0) & (right >= 0), weight, 0).astype(jnp.float32)
            span = (rows_of(i), slice(j * B, (j + 1) * B))
            front_ref[span] = front_ref[span] - weight * product[span]

    for k in range(4):
        for d in range(1, NX):
            x_copy(k, d).wait_send()
    for part in range(3):
        z_copy(part).wait_send()

    @pl.when(r > 0)
    def _():
        inverse_copy().wait_send()

    for j in range(SH):

        @pl.when(r == 0)
        def _():
            for d in range(1, 4):
                r_copy(j, d).wait_send()

        @pl.when(r > 1)
        def _():
            c_copy(j, 0).wait_send()

        for d in range(1, NY):
            y_copy(j, d).wait_send()
            c_copy(j, d).wait_send()

        @pl.when(lax.rem(c + j, NX) > 0)
        def _():
            n_copy(j).wait_send()

        f_copy(j).wait_send()
        for b in range(2):
            for d in range(1, NY):
                p_copy(b, j, d).wait_send()


def per_device(children, child_map, panel_inverse, pattern):
    anywhere = pl.BlockSpec(memory_space=pl.ANY)
    smem = pl.BlockSpec(memory_space=pltpu.SMEM)
    vmem = pl.BlockSpec(memory_space=pltpu.VMEM)
    pack, rows, cols = pl.pallas_call(
        pack_kernel,
        name="pack",
        out_shape=(
            jax.ShapeDtypeStruct((2, GROUPS, SLOTS, B), jnp.float32),
            jax.ShapeDtypeStruct((2 * NX * PB,), jnp.int32),
            jax.ShapeDtypeStruct((2 * NX * 4,), jnp.int32),
        ),
        in_specs=[smem, anywhere],
        out_specs=(anywhere, smem, smem),
        scratch_shapes=[
            pltpu.VMEM((CB * B, CB * B), jnp.float32),
            pltpu.SemaphoreType.DMA((4,)),
            pltpu.SemaphoreType.DMA((2, CB)),
        ],
        compiler_params=pltpu.CompilerParams(vmem_limit_bytes=60 * 2**20),
    )(child_map, children[0])
    pack = pack.reshape(2, GROUPS, TILES, B, B)
    f32, bf16 = jnp.float32, jnp.bfloat16
    dma = pltpu.SemaphoreType.DMA
    chunk = pltpu.VMEM((ZERO + 1, B, B), f32)
    return pl.pallas_call(
        front_kernel,
        name="front",
        out_shape=(
            jax.ShapeDtypeStruct((BIG, WIDTH), f32),
            jax.ShapeDtypeStruct((256, WIDTH), f32),
        ),
        in_specs=[smem, smem, smem, anywhere, anywhere],
        out_specs=(vmem, vmem),
        scratch_shapes=[
            chunk, chunk, chunk, chunk,
            pltpu.VMEM((BIG, WIDTH), f32), pltpu.VMEM((BIG, WIDTH), f32),
            pltpu.VMEM((BIG, WIDTH), f32), pltpu.VMEM((18 * B, WIDTH), f32),
            pltpu.VMEM((NY * WIDTH, W), f32),
            pltpu.VMEM((NY * WIDTH, W), bf16), pltpu.VMEM((NY * WIDTH, W), bf16),
            pltpu.VMEM((WIDTH, W), f32), pltpu.VMEM((WIDTH, W), f32),
            pltpu.VMEM((W, W), f32),
            pltpu.VMEM((W, WIDTH), bf16), pltpu.VMEM((W, WIDTH), bf16),
            dma((12,)), dma((12,)), dma((4,)), dma((3,)), dma((3,)), dma(()), dma((3,)), dma(()),
            dma((9,)), dma((3,)), dma((12,)), dma((12,)), dma((9,)), dma((9,)), dma((3,)), dma((3,)), dma((3,)), dma((3,)), dma((3,)),
            dma((18,)), dma((18,)), pltpu.SemaphoreType.REGULAR,
        ],
        compiler_params=pltpu.CompilerParams(
            collective_id=1, has_side_effects=True, vmem_limit_bytes=62 * 2**20
        ),
    )(rows, cols, pattern, pack, panel_inverse)


def solution(mesh):
    placed = (P("grp", "row", "col"), P(), P("row", None), P())
    return jax.shard_map(
        per_device,
        mesh=mesh,
        in_specs=placed,
        out_specs=(P("row", ("grp", "col")), P("row", ("grp", "col"))),
        check_vma=False,
    )
```

```python
import functools

import jax
import jax.numpy as jnp
from jax import lax
from jax.experimental import pallas as pl
from jax.experimental.pallas import tpu as pltpu
from jax.sharding import PartitionSpec as P

MESH = pl.DeviceIdType.MESH
B = 128
GROUPS = 8
PB = 24
CB = 12
SH = 3
WT = 8
W = 1024
NX = 4
NY = 4
HALF = 6
HROWS = HALF * B
SLOTS = 2 * HROWS
TILES = 2 * HALF
ZERO = NX * 2 * HALF
NONE = 1000
WIDTH = SH * B
BIG = 3072


def front_kernel(
    map_ref, child_ref, inverse_ref,
    sum_ref, product_ref, panel_ref,
    rows_ref, cols_ref, held, staged,
    as_ref, ao_ref, bs_ref, bo_ref,
    out_part, in_part, product_out,
    own, own_hi, own_lo, near, far,
    inverse_all, top_hi, top_lo,
    held_sem, x_send, x_recv, z_send, z_recv, i_send, i_recv, i_local,
    r_send, r_recv, c_send, c_recv, y_send, y_recv, n_send, n_recv, n_local, f_send, f_recv,
    p_send, p_recv, p_local, sum_sem, go,
):
    g = lax.axis_index("grp")
    r = lax.axis_index("row")
    c = lax.axis_index("col")
    x, zh = g // 2, lax.rem(g, 2)

    def at(grp=None, row=None, col=None):
        return {
            "grp": g if grp is None else grp,
            "row": r if row is None else row,
            "col": c if col is None else col,
        }

    def x_peer(d):
        return at(grp=lax.rem(x + d, NX) * 2 + zh)

    def y_peer(d):
        return at(col=lax.rem(c + d, NY))

    z_peer = at(grp=2 * x + 1 - zh)

    def held_copy(h, q):
        return pltpu.make_async_copy(
            child_ref.at[pl.ds(h * HALF, HALF), :, pl.ds(q * B, B)], held.at[q], held_sem.at[h, q]
        )

    for q in range(CB):
        held_copy(0, q).start()
    core = lax.rem(r, 2)
    other_core = at(row=r + 1 - 2 * core)

    barrier = pltpu.get_barrier_semaphore()
    peers = [x_peer(d) for d in range(1, NX)] + [y_peer(d) for d in range(1, NY)]
    peers += [at(row=lax.rem(r + d, 4)) for d in range(1, 4)] + [z_peer]
    for peer in peers:
        pl.semaphore_signal(barrier, inc=1, device_id=peer, device_id_type=MESH)
    pl.semaphore_wait(barrier, len(peers))

    def remote(src, dst, send, recv, device):
        return pltpu.make_async_remote_copy(
            src_ref=src, dst_ref=dst, send_sem=send, recv_sem=recv,
            device_id=device, device_id_type=MESH,
        )

    chunks = [as_ref, ao_ref, bs_ref, bo_ref]

    def x_copy(k, d):
        return remote(
            staged.at[k, d - 1],
            chunks[k].at[pl.ds(x * TILES, TILES)],
            x_send.at[k * 3 + d - 1], x_recv.at[k * 3 + d - 1], x_peer(d),
        )

    def x_arrival(k, d):
        source = lax.rem(x + NX - d, NX)
        return remote(
            staged.at[k, d - 1],
            chunks[k].at[pl.ds(source * TILES, TILES)],
            x_send.at[k * 3 + d - 1], x_recv.at[k * 3 + d - 1], x_peer(NX - d),
        )

    def pack(k):
        places = []
        for d in range(NX):
            owner = lax.rem(x + d, NX) * 2 + (zh if k % 2 == 0 else 1 - zh)
            low = c * PB + owner * SH
            before = sum((map_ref[g, c * CB + q] < low).astype(jnp.int32) for q in range(CB))
            for slot in range(2):
                places.append((d, slot, jnp.minimum(before + slot, CB - 1)))

        @pl.loop(0, HALF)
        def _(a):
            for d, slot, q in places:
                if d == 0:
                    chunks[k][x * TILES + slot * HALF + a] = held[q, a]
                else:
                    staged[k, d - 1, slot * HALF + a] = held[q, a]

    def x_start(k):
        for d in (2, 1, 3):
            x_copy(k, d).start()

    def x_wait(k):
        for d in range(1, NX):
            x_arrival(k, d).wait_recv()

    def inverse_copy():
        return remote(
            inverse_ref,
            inverse_all.at[pl.ds(pl.multiple_of(r * 256, 256), 256), :],
            i_send, i_recv.at[r - 1], at(row=0),
        )

    for ref in chunks:
        ref[ZERO] = jnp.zeros((B, B), jnp.float32)

    @pl.when(r == 0)
    def _():
        pltpu.make_async_copy(inverse_ref, inverse_all.at[pl.ds(0, 256), :], i_local).start()

    for q in range(CB):
        held_copy(0, q).wait()
    pack(1)

    @pl.when(core == 0)
    def _():
        x_start(1)

    pack(0)

    @pl.when(r == 0)
    def _():
        x_start(0)

    for q in range(CB):
        held_copy(1, q).start()

    @pl.when(r > 0)
    def _():
        inverse_copy().start()

    for n in range(NX):
        child = 2 * n + zh

        def place_row(i, at_tile):
            found = map_ref[child, r * CB + jnp.minimum(at_tile, CB - 1)] == r * PB + i
            hit = found & (at_tile < CB)
            rows_ref[n * PB + i] = jnp.where(hit & (at_tile < HALF), at_tile, NONE)
            rows_ref[(NX + n) * PB + i] = jnp.where(hit & (at_tile >= HALF), at_tile - HALF, NONE)
            return at_tile + hit.astype(jnp.int32)

        lax.fori_loop(0, PB, place_row, jnp.int32(0))
        for d in range(2):
            low = c * PB + (2 * x + (zh if d == 0 else 1 - zh)) * SH
            slot = jnp.int32(0)
            for j in range(SH):
                hit = sum(
                    (map_ref[child, c * CB + q] == low + j).astype(jnp.int32) for q in range(CB)
                )
                cols_ref[(d * NX + n) * 4 + j] = jnp.where(hit > 0, (n * 2 + slot) * HALF, NONE)
                slot = slot + hit

    for q in range(CB):
        held_copy(1, q).wait()
    pack(3)
    pack(2)

    def tile(d, i, j, use):
        total = None
        for s in range(NX):
            for h, ref in use:
                index = jnp.minimum(
                    rows_ref[h * NX * PB + s * PB + i] + cols_ref[d * NX * 4 + s * 4 + j], ZERO
                )
                value = ref[index]
                total = value if total is None else total + value
        return total

    def spread(first, last, d, put):
        a_ref, b_ref = (as_ref, bs_ref) if d == 0 else (ao_ref, bo_ref)
        for low, high, use in (
            (0, 9, ((0, a_ref),)),
            (9, 15, ((0, a_ref), (1, b_ref))),
            (15, 24, ((1, b_ref),)),
        ):
            low, high = max(low, first), min(high, last)
            if low < high:

                @pl.loop(low, high)
                def _(i):
                    for j in range(SH):
                        put(i, j, tile(d, i, j, use))

    def rows_of(i):
        return pl.ds(pl.multiple_of(i * B, B), B)

    def put_out(i, j, value):
        out_part[rows_of(i), j * B : (j + 1) * B] = value

    def z_copy(part):
        span = pl.ds(part * W, W)
        return remote(
            out_part.at[span, :], in_part.at[span, :],
            z_send.at[part], z_recv.at[part], z_peer,
        )

    def own_tile(ref, col, j):
        return ref.at[pl.ds(pl.multiple_of(col * WIDTH + j * B, B), B), :]

    def own_half(col, j, k):
        start = col * WIDTH + j * B + k * (B // 2)
        return own.at[pl.ds(pl.multiple_of(start, B // 2), B // 2), :]

    def r_copy(j, d):
        part = own_tile(own, c, j) if d == 1 else own_half(c, j, d - 2)
        return remote(part, part, r_send.at[(d - 1) * 3 + j], r_recv.at[j], at(row=d))

    def c_copy(j, d):
        part = own_half(lax.rem(c + NY - d, NY), j, core)
        return remote(part, part, c_send.at[d * 3 + j], c_recv.at[d * 3 + j], other_core)

    def c_arrival(j, d):
        part = own_half(lax.rem(c + NY - d, NY), j, 1 - core)
        return remote(part, part, c_send.at[d * 3 + j], c_recv.at[d * 3 + j], other_core)

    def y_copy(j, d):
        part = own_half(c, j, core)
        n = (d - 1) * 3 + j
        return remote(part, part, y_send.at[n], y_recv.at[n], y_peer(d))

    def y_arrival(j, d):
        part = own_half(lax.rem(c + NY - d, NY), j, core)
        n = (d - 1) * 3 + j
        return remote(part, part, y_send.at[n], y_recv.at[n], y_peer(NY - d))

    @pl.when(r == 0)
    def _():
        x_wait(1)
        spread(0, WT, 1, put_out)
        z_copy(0).start()
        x_wait(0)
        x_start(3)

        z_copy(0).wait_recv()

        def put_top(i, j, value):
            span = (rows_of(i), slice(j * B, (j + 1) * B))
            in_part[span] = in_part[span] + value

        spread(0, WT, 0, put_top)
        for k in range(1, 4):
            remote(
                inverse_ref, inverse_all.at[pl.ds(k * 256, 256), :],
                i_send, i_recv.at[k - 1], at(row=k),
            ).wait_recv()
        pltpu.make_async_copy(inverse_ref, inverse_all.at[pl.ds(0, 256), :], i_local).wait()

        @pl.loop(0, WT)
        def _(i):
            value = in_part[rows_of(i), :]
            high = value.astype(jnp.bfloat16)
            top_hi[rows_of(i), :] = high
            top_lo[rows_of(i), :] = (value - high.astype(jnp.float32)).astype(jnp.bfloat16)

        for k in range(4):
            block = inverse_all[k * 256 : (k + 1) * 256, :]
            high = block.astype(jnp.bfloat16)
            low = (block - high.astype(jnp.float32)).astype(jnp.bfloat16)
            dot = functools.partial(jnp.dot, preferred_element_type=jnp.float32)
            part = dot(high, top_lo[...]) + dot(low, top_hi[...]) + dot(high, top_hi[...])
            own[pl.ds(pl.multiple_of(c * WIDTH, WIDTH), WIDTH), k * 256 : (k + 1) * 256] = part.T
        for j in range(SH):
            r_copy(j, 2).start()
            r_copy(j, 3).start()
            r_copy(j, 1).start()
            for d in range(1, NY):
                y_copy(j, d).start()
        x_wait(3)
        pl.semaphore_signal(go, inc=1, device_id=other_core, device_id_type=MESH)

    def take(d):
        for j in range(SH):
            part = own_tile(own, c, j) if d == 1 else own_half(c, j, core)
            remote(part, part, r_send.at[j], r_recv.at[j], at(row=0)).wait_recv()
            for d2 in range(1, NY):
                y_copy(j, d2).start()
            if d > 1:
                c_copy(j, 0).start()

    @pl.when(core == 1)
    def _():
        pl.semaphore_wait(go, 1)
        x_start(1)
        x_start(3)

    @pl.when(r == 2)
    def _():
        x_wait(1)
        pl.semaphore_signal(go, inc=1, device_id=other_core, device_id_type=MESH)
        x_start(3)
        spread(0, WT, 1, put_out)
        z_copy(0).start()
        x_wait(3)
        x_start(0)

    @pl.when(r == 1)
    def _():
        take(1)

    @pl.when(core == 1)
    def _():
        x_wait(1)
        spread(0, WT, 1, put_out)
        z_copy(0).start()

    @pl.when(r == 3)
    def _():
        take(3)

    @pl.when(core == 1)
    def _():
        x_wait(3)

    spread(WT, PB, 1, put_out)

    @pl.when(r != 1)
    def _():
        z_copy(1).start()

    @pl.when(core == 0)
    def _():
        z_copy(2).start()

    @pl.when(r == 2)
    def _():
        take(2)

    @pl.when(r > 1)
    def _():
        for j in range(SH):
            c_arrival(j, 0).wait_recv()

    def n_copy(j):
        return remote(
            own_tile(own, r, j), near.at[pl.ds(j * B, B), :],
            n_send.at[j], n_recv.at[j], at(grp=lax.rem(x + 2 * NX - c - j, NX) * 2 + zh),
        )

    def n_arrival(j):
        return remote(
            own_tile(own, r, j), near.at[pl.ds(j * B, B), :],
            n_send.at[j], n_recv.at[j], at(grp=lax.rem(x + c + j, NX) * 2 + zh),
        )

    def n_own(j):
        return pltpu.make_async_copy(own_tile(own, r, j), near.at[pl.ds(j * B, B), :], n_local.at[j])

    def f_copy(j):
        return remote(
            near.at[pl.ds(j * B, B), :], far.at[pl.ds(j * B, B), :],
            f_send.at[j], f_recv.at[j], z_peer,
        )

    for j in range(SH):
        for d in (1, 3, 2):
            y_arrival(j, d).wait_recv()
            c_copy(j, d).start()
        for d in range(1, NY):

            @pl.when(lax.rem(c + NY - r, NY) == d)
            def _():
                c_arrival(j, d).wait_recv()

        @pl.when(lax.rem(c + j, NX) > 0)
        def _():
            n_copy(j).start()

        @pl.when(lax.rem(c + j, NX) == 0)
        def _():
            n_own(j).start()

    @pl.when(core == 1)
    def _():
        x_start(0)

    x_start(2)

    for j in range(SH):

        @pl.when(lax.rem(c + j, NX) > 0)
        def _():
            n_arrival(j).wait_recv()

        @pl.when(lax.rem(c + j, NX) == 0)
        def _():
            n_own(j).wait()

        f_copy(j).start()

    @pl.when(r == 1)
    def _():
        z_copy(1).start()

    @pl.when(core == 1)
    def _():
        z_copy(2).start()

    for j in range(SH):
        for d in range(1, NY):

            @pl.when(lax.rem(c + NY - r, NY) != d)
            def _():
                c_arrival(j, d).wait_recv()

    @pl.loop(0, NY * SH)
    def _(t):
        value = own[rows_of(t), :]
        high = value.astype(jnp.bfloat16)
        own_hi[rows_of(t), :] = high
        own_lo[rows_of(t), :] = (value - high.astype(jnp.float32)).astype(jnp.bfloat16)

    def place(b, j):
        return 3 * (2 * lax.rem(x + c + j, NX) + (zh if b == 0 else 1 - zh)) + j

    def p_copy(b, j, d):
        n = (b * 3 + j) * 3 + d - 1
        return remote(
            product_out.at[pl.ds(n * B, B), :], product_ref.at[rows_of(place(b, j)), :],
            p_send.at[n], p_recv.at[n], y_peer(d),
        )

    def p_arrival(b, j, d):
        n = (b * 3 + j) * 3 + d - 1
        source = lax.rem(c + NY - d, NY)
        index = 3 * (2 * lax.rem(x + source + j, NX) + (zh if b == 0 else 1 - zh)) + j
        return remote(
            product_out.at[pl.ds(n * B, B), :], product_ref.at[rows_of(index), :],
            p_send.at[n], p_recv.at[n], y_peer(NY - d),
        )

    def p_own(b, j):
        n = 18 + b * 3 + j
        return pltpu.make_async_copy(
            product_out.at[pl.ds(n * B, B), :], product_ref.at[rows_of(place(b, j)), :],
            p_local.at[b * 3 + j],
        )

    def times(a, b):
        return lax.dot_general(a, b, (((1,), (1,)), ((), ())), preferred_element_type=jnp.float32)

    for b in range(2):
        for j in range(SH):
            if b == 1:
                f_copy(j).wait_recv()
            value = (near, far)[b][j * B : (j + 1) * B, :]
            high = value.astype(jnp.bfloat16)
            low = (value - high.astype(jnp.float32)).astype(jnp.bfloat16)
            for d in (2, 1, 3, 0):
                col = lax.rem(c + d, NY)
                span = pl.ds(pl.multiple_of(col * WIDTH, WIDTH), WIDTH)
                got = (
                    times(high, own_lo[span, :]) + times(low, own_hi[span, :])
                    + times(high, own_hi[span, :])
                )
                n = 18 + b * 3 + j if d == 0 else (b * 3 + j) * 3 + d - 1
                product_out[n * B : (n + 1) * B, :] = got
                if d == 0:
                    p_own(b, j).start()
                else:
                    p_copy(b, j, d).start()

    panel_ref[...] = own[
        pl.ds(pl.multiple_of(c * WIDTH, WIDTH), WIDTH), pl.ds(pl.multiple_of(r * 256, 256), 256)
    ].T

    @pl.when(r > 0)
    def _():
        x_wait(0)

    x_wait(2)

    def sum_copy(part):
        span = pl.ds(part * W, W)
        return pltpu.make_async_copy(out_part.at[span, :], sum_ref.at[span, :], sum_sem.at[part])

    def put_sum(i, j, value):
        span = (rows_of(i), slice(j * B, (j + 1) * B))
        out_part[span] = value + in_part[span]

    for part in range(3):
        z_copy(part).wait_send()
        if part > 0:
            z_copy(part).wait_recv()
            spread(part * WT, (part + 1) * WT, 0, put_sum)
        else:

            @pl.when(r == 0)
            def _():
                out_part[0:W, :] = in_part[0:W, :]

            @pl.when(r > 0)
            def _():
                z_copy(0).wait_recv()
                spread(0, WT, 0, put_sum)

        sum_copy(part).start()

    for b in range(2):
        for j in range(SH):
            for d in range(1, NY):
                p_arrival(b, j, d).wait_recv()
            p_own(b, j).wait()
    for part in range(3):
        sum_copy(part).wait()

    for k in range(4):
        for d in range(1, NX):
            x_copy(k, d).wait_send()

    @pl.when(r > 0)
    def _():
        inverse_copy().wait_send()

    for j in range(SH):

        @pl.when(r == 0)
        def _():
            for d in range(1, 4):
                r_copy(j, d).wait_send()

        @pl.when(r > 1)
        def _():
            c_copy(j, 0).wait_send()

        for d in range(1, NY):
            y_copy(j, d).wait_send()
            c_copy(j, d).wait_send()

        @pl.when(lax.rem(c + j, NX) > 0)
        def _():
            n_copy(j).wait_send()

        f_copy(j).wait_send()
        for b in range(2):
            for d in range(1, NY):
                p_copy(b, j, d).wait_send()


def update_kernel(pattern_ref, sum_ref, product_ref, panel_in, front_ref, panel_ref):
    step = pl.program_id(0)
    r = lax.axis_index("row")
    panel_ref[...] = panel_in[...]
    for i in range(SH):
        for j in range(SH):
            down = r * PB + step * SH + i - WT
            right = lax.axis_index("col") * PB + lax.axis_index("grp") * SH + j - WT
            weight = pattern_ref[jnp.maximum(down, 0), jnp.maximum(right, 0)]
            weight = jnp.where((down >= 0) & (right >= 0), weight, 0).astype(jnp.float32)
            span = (slice(i * B, (i + 1) * B), slice(j * B, (j + 1) * B))
            front_ref[span] = sum_ref[span] - weight * product_ref[span]


def per_device(children, child_map, panel_inverse, pattern):
    anywhere = pl.BlockSpec(memory_space=pl.ANY)
    smem = pl.BlockSpec(memory_space=pltpu.SMEM)
    vmem = pl.BlockSpec(memory_space=pltpu.VMEM)
    f32, bf16 = jnp.float32, jnp.bfloat16
    dma = pltpu.SemaphoreType.DMA
    chunk = pltpu.VMEM((ZERO + 1, B, B), f32)
    sums, product, panel = pl.pallas_call(
        front_kernel,
        name="front",
        out_shape=(
            jax.ShapeDtypeStruct((BIG, WIDTH), f32),
            jax.ShapeDtypeStruct((BIG, WIDTH), f32),
            jax.ShapeDtypeStruct((256, WIDTH), f32),
        ),
        in_specs=[smem, anywhere, anywhere],
        out_specs=(anywhere, anywhere, vmem),
        scratch_shapes=[
            pltpu.SMEM((2 * NX * PB,), jnp.int32), pltpu.SMEM((2 * NX * 4,), jnp.int32),
            pltpu.VMEM((CB, HALF, B, B), f32), pltpu.VMEM((4, NX - 1, TILES, B, B), f32),
            chunk, chunk, chunk, chunk,
            pltpu.VMEM((BIG, WIDTH), f32), pltpu.VMEM((BIG, WIDTH), f32),
            pltpu.VMEM((24 * B, WIDTH), f32),
            pltpu.VMEM((NY * WIDTH, W), f32),
            pltpu.VMEM((NY * WIDTH, W), bf16), pltpu.VMEM((NY * WIDTH, W), bf16),
            pltpu.VMEM((WIDTH, W), f32), pltpu.VMEM((WIDTH, W), f32),
            pltpu.VMEM((W, W), f32),
            pltpu.VMEM((W, WIDTH), bf16), pltpu.VMEM((W, WIDTH), bf16),
            dma((2, CB)), dma((12,)), dma((12,)), dma((3,)), dma((3,)), dma(()), dma((3,)), dma(()),
            dma((9,)), dma((3,)), dma((12,)), dma((12,)), dma((9,)), dma((9,)),
            dma((3,)), dma((3,)), dma((3,)), dma((3,)), dma((3,)),
            dma((18,)), dma((18,)), dma((6,)), dma((3,)), pltpu.SemaphoreType.REGULAR,
        ],
        compiler_params=pltpu.CompilerParams(
            collective_id=1, has_side_effects=True, vmem_limit_bytes=63 * 2**20
        ),
    )(child_map, children.reshape(CB, B, CB * B), panel_inverse)
    rows = SH * B
    block = pl.BlockSpec((rows, WIDTH), lambda i: (i, 0))
    part = pl.BlockSpec((256 // GROUPS, WIDTH), lambda i: (i, 0))
    return pl.pallas_call(
        update_kernel,
        name="update",
        grid=(BIG // rows,),
        out_shape=(
            jax.ShapeDtypeStruct((BIG, WIDTH), f32),
            jax.ShapeDtypeStruct((256, WIDTH), f32),
        ),
        in_specs=[smem, block, block, part],
        out_specs=(block, part),
        compiler_params=pltpu.CompilerParams(vmem_limit_bytes=60 * 2**20),
    )(pattern, sums, product, panel)


def solution(mesh):
    placed = (P("grp", "row", "col"), P(), P("row", None), P())
    return jax.shard_map(
        per_device,
        mesh=mesh,
        in_specs=placed,
        out_specs=(P("row", ("grp", "col")), P("row", ("grp", "col"))),
        check_vma=False,
    )
```

```python
import jax
import jax.numpy as jnp
from jax import lax
from jax.experimental import pallas as pl
from jax.experimental.pallas import tpu as pltpu
from jax.sharding import PartitionSpec as P

MESH = pl.DeviceIdType.MESH
B = 128
GROUPS = 8
PB = 24
CB = 12
SH = 3
WT = 8
W = 1024
NX = 4
NY = 4
HALF = 6
HROWS = HALF * B
SLOTS = 2 * HROWS
TILES = 2 * HALF
ZERO = NX * 2 * HALF
NONE = 1000
WIDTH = SH * B
BIG = 3072
STEPS = 2


def front_kernel(
    map_ref, child_ref, inverse_ref,
    sum_ref, product_ref, panel_ref,
    rows_ref, cols_ref, held, staged,
    as_ref, ao_ref, bs_ref, bo_ref,
    out_part, in_part, product_out,
    own, own_hi, own_lo, near, far,
    inverse_all,
    held_sem, x_send, x_recv, z_send, z_recv, i_send, i_recv, i_local,
    r_send, r_recv, c_send, c_recv, y_send, y_recv, n_send, n_recv, n_local, f_send, f_recv,
    p_send, p_recv, p_local, sum_sem, go,
):
    g = lax.axis_index("grp")
    r = lax.axis_index("row")
    c = lax.axis_index("col")
    x, zh = g // 2, lax.rem(g, 2)

    def at(grp=None, row=None, col=None):
        return {
            "grp": g if grp is None else grp,
            "row": r if row is None else row,
            "col": c if col is None else col,
        }

    def x_peer(d):
        return at(grp=lax.rem(x + d, NX) * 2 + zh)

    def y_peer(d):
        return at(col=lax.rem(c + d, NY))

    z_peer = at(grp=2 * x + 1 - zh)

    def held_copy(h, q):
        return pltpu.make_async_copy(
            child_ref.at[pl.ds(h * HALF, HALF), :, pl.ds(q * B, B)], held.at[q], held_sem.at[h, q]
        )

    for q in range(CB):
        held_copy(0, q).start()
    core = lax.rem(r, 2)
    other_core = at(row=r + 1 - 2 * core)

    barrier = pltpu.get_barrier_semaphore()
    peers = [x_peer(d) for d in range(1, NX)] + [y_peer(d) for d in range(1, NY)]
    peers += [at(row=lax.rem(r + d, 4)) for d in range(1, 4)] + [z_peer]
    for peer in peers:
        pl.semaphore_signal(barrier, inc=1, device_id=peer, device_id_type=MESH)
    pl.semaphore_wait(barrier, len(peers))

    def remote(src, dst, send, recv, device):
        return pltpu.make_async_remote_copy(
            src_ref=src, dst_ref=dst, send_sem=send, recv_sem=recv,
            device_id=device, device_id_type=MESH,
        )

    chunks = [as_ref, ao_ref, bs_ref, bo_ref]

    def x_copy(k, d):
        return remote(
            staged.at[k, d - 1],
            chunks[k].at[pl.ds(x * TILES, TILES)],
            x_send.at[k * 3 + d - 1], x_recv.at[k * 3 + d - 1], x_peer(d),
        )

    def x_arrival(k, d):
        source = lax.rem(x + NX - d, NX)
        return remote(
            staged.at[k, d - 1],
            chunks[k].at[pl.ds(source * TILES, TILES)],
            x_send.at[k * 3 + d - 1], x_recv.at[k * 3 + d - 1], x_peer(NX - d),
        )

    def pack(k):
        places = []
        for d in range(NX):
            owner = lax.rem(x + d, NX) * 2 + (zh if k % 2 == 0 else 1 - zh)
            low = c * PB + owner * SH
            before = sum((map_ref[g, c * CB + q] < low).astype(jnp.int32) for q in range(CB))
            for slot in range(2):
                places.append((d, slot, jnp.minimum(before + slot, CB - 1)))

        @pl.loop(0, HALF)
        def _(a):
            for d, slot, q in places:
                if d == 0:
                    chunks[k][x * TILES + slot * HALF + a] = held[q, a]
                else:
                    staged[k, d - 1, slot * HALF + a] = held[q, a]

    def x_start(k):
        for d in (2, 1, 3):
            x_copy(k, d).start()

    def x_wait(k):
        for d in range(1, NX):
            x_arrival(k, d).wait_recv()

    def inverse_copy():
        return remote(
            inverse_ref,
            inverse_all.at[pl.ds(pl.multiple_of(r * 256, 256), 256), :],
            i_send, i_recv.at[r - 1], at(row=0),
        )

    for ref in chunks:
        ref[ZERO] = jnp.zeros((B, B), jnp.float32)

    @pl.when(r == 0)
    def _():
        pltpu.make_async_copy(inverse_ref, inverse_all.at[pl.ds(0, 256), :], i_local).start()

    for q in range(CB):
        held_copy(0, q).wait()
    pack(1)

    @pl.when(core == 0)
    def _():
        x_start(1)

    pack(0)

    @pl.when(r == 0)
    def _():
        x_start(0)

    for q in range(CB):
        held_copy(1, q).start()

    @pl.when(r > 0)
    def _():
        inverse_copy().start()

    for n in range(NX):
        child = 2 * n + zh

        def place_row(i, at_tile):
            found = map_ref[child, r * CB + jnp.minimum(at_tile, CB - 1)] == r * PB + i
            hit = found & (at_tile < CB)
            rows_ref[n * PB + i] = jnp.where(hit & (at_tile < HALF), at_tile, NONE)
            rows_ref[(NX + n) * PB + i] = jnp.where(hit & (at_tile >= HALF), at_tile - HALF, NONE)
            return at_tile + hit.astype(jnp.int32)

        lax.fori_loop(0, PB, place_row, jnp.int32(0))
        for d in range(2):
            low = c * PB + (2 * x + (zh if d == 0 else 1 - zh)) * SH
            slot = jnp.int32(0)
            for j in range(SH):
                hit = sum(
                    (map_ref[child, c * CB + q] == low + j).astype(jnp.int32) for q in range(CB)
                )
                cols_ref[(d * NX + n) * 4 + j] = jnp.where(hit > 0, (n * 2 + slot) * HALF, NONE)
                slot = slot + hit

    for q in range(CB):
        held_copy(1, q).wait()
    pack(3)
    pack(2)

    def tile(d, i, j, use):
        total = None
        for s in range(NX):
            for h, ref in use:
                index = jnp.minimum(
                    rows_ref[h * NX * PB + s * PB + i] + cols_ref[d * NX * 4 + s * 4 + j], ZERO
                )
                value = ref[index]
                total = value if total is None else total + value
        return total

    def spread(first, last, d, put):
        a_ref, b_ref = (as_ref, bs_ref) if d == 0 else (ao_ref, bo_ref)
        for low, high, use in (
            (0, 9, ((0, a_ref),)),
            (9, 15, ((0, a_ref), (1, b_ref))),
            (15, 24, ((1, b_ref),)),
        ):
            low, high = max(low, first), min(high, last)
            if low < high:

                @pl.loop(low, high)
                def _(i):
                    for j in range(SH):
                        put(i, j, tile(d, i, j, use))

    def rows_of(i):
        return pl.ds(pl.multiple_of(i * B, B), B)

    def put_out(i, j, value):
        out_part[rows_of(i), j * B : (j + 1) * B] = value

    def z_copy(part):
        span = pl.ds(part * W, W)
        return remote(
            out_part.at[span, :], in_part.at[span, :],
            z_send.at[part], z_recv.at[part], z_peer,
        )

    def own_tile(ref, col, j):
        return ref.at[pl.ds(pl.multiple_of(col * WIDTH + j * B, B), B), :]

    def own_half(col, j, k):
        start = col * WIDTH + j * B + k * (B // 2)
        return own.at[pl.ds(pl.multiple_of(start, B // 2), B // 2), :]

    def r_copy(j, d):
        part = own_tile(own, c, j) if d == 1 else own_half(c, j, d - 2)
        return remote(part, part, r_send.at[(d - 1) * 3 + j], r_recv.at[j], at(row=d))

    def c_copy(j, d):
        part = own_half(lax.rem(c + NY - d, NY), j, core)
        return remote(part, part, c_send.at[d * 3 + j], c_recv.at[d * 3 + j], other_core)

    def c_arrival(j, d):
        part = own_half(lax.rem(c + NY - d, NY), j, 1 - core)
        return remote(part, part, c_send.at[d * 3 + j], c_recv.at[d * 3 + j], other_core)

    def y_copy(j, d):
        part = own_half(c, j, core)
        n = (d - 1) * 3 + j
        return remote(part, part, y_send.at[n], y_recv.at[n], y_peer(d))

    def y_arrival(j, d):
        part = own_half(lax.rem(c + NY - d, NY), j, core)
        n = (d - 1) * 3 + j
        return remote(part, part, y_send.at[n], y_recv.at[n], y_peer(NY - d))

    def times(a, b):
        return lax.dot_general(a, b, (((1,), (1,)), ((), ())), preferred_element_type=jnp.float32)

    @pl.when(r == 0)
    def _():
        x_wait(1)
        spread(0, WT, 1, put_out)
        z_copy(0).start()
        for k in range(1, 4):
            remote(
                inverse_ref, inverse_all.at[pl.ds(k * 256, 256), :],
                i_send, i_recv.at[k - 1], at(row=k),
            ).wait_recv()
        pltpu.make_async_copy(inverse_ref, inverse_all.at[pl.ds(0, 256), :], i_local).wait()

        @pl.loop(0, WT)
        def _(i):
            value = inverse_all[rows_of(i), :]
            high = value.astype(jnp.bfloat16)
            own_hi[rows_of(i), :] = high
            own_lo[rows_of(i), :] = (value - high.astype(jnp.float32)).astype(jnp.bfloat16)

        x_wait(0)
        x_start(3)

        z_copy(0).wait_recv()

        def put_top(i, j, value):
            span = (rows_of(i), slice(j * B, (j + 1) * B))
            in_part[span] = in_part[span] + value

        spread(0, WT, 0, put_top)
        top = slice(W, W + WIDTH)
        for i in range(WT):
            value = in_part[i * B : (i + 1) * B, :].T
            high = value.astype(jnp.bfloat16)
            own_hi[top, i * B : (i + 1) * B] = high
            own_lo[top, i * B : (i + 1) * B] = (value - high.astype(jnp.float32)).astype(jnp.bfloat16)
        for k in range(4):
            part = slice(k * 256, (k + 1) * 256)
            own[pl.ds(pl.multiple_of(c * WIDTH, WIDTH), WIDTH), part] = (
                times(own_hi[top, :], own_lo[part, :])
                + times(own_lo[top, :], own_hi[part, :])
                + times(own_hi[top, :], own_hi[part, :])
            )
        for j in range(SH):
            r_copy(j, 2).start()
            r_copy(j, 3).start()
            r_copy(j, 1).start()
            for d in range(1, NY):
                y_copy(j, d).start()
        x_wait(3)
        pl.semaphore_signal(go, inc=1, device_id=other_core, device_id_type=MESH)

    def take(d):
        for j in range(SH):
            part = own_tile(own, c, j) if d == 1 else own_half(c, j, core)
            remote(part, part, r_send.at[j], r_recv.at[j], at(row=0)).wait_recv()
            for d2 in range(1, NY):
                y_copy(j, d2).start()
            if d > 1:
                c_copy(j, 0).start()

    @pl.when(core == 1)
    def _():
        pl.semaphore_wait(go, 1)
        x_start(1)
        x_start(3)

    @pl.when(r == 2)
    def _():
        x_wait(1)
        pl.semaphore_signal(go, inc=1, device_id=other_core, device_id_type=MESH)
        x_start(3)
        spread(0, WT, 1, put_out)
        z_copy(0).start()
        x_wait(3)
        x_start(0)

    @pl.when(r == 1)
    def _():
        take(1)

    @pl.when(core == 1)
    def _():
        x_wait(1)
        spread(0, WT, 1, put_out)
        z_copy(0).start()

    @pl.when(r == 3)
    def _():
        take(3)

    @pl.when(core == 1)
    def _():
        x_wait(3)

    spread(WT, PB, 1, put_out)

    z_copy(1).start()

    @pl.when(core == 0)
    def _():
        z_copy(2).start()

    @pl.when(r == 2)
    def _():
        take(2)

    @pl.when(r > 1)
    def _():
        for j in range(SH):
            c_arrival(j, 0).wait_recv()

    def n_copy(j):
        return remote(
            own_tile(own, r, j), near.at[pl.ds(j * B, B), :],
            n_send.at[j], n_recv.at[j], at(grp=lax.rem(x + 2 * NX - c - j, NX) * 2 + zh),
        )

    def n_arrival(j):
        return remote(
            own_tile(own, r, j), near.at[pl.ds(j * B, B), :],
            n_send.at[j], n_recv.at[j], at(grp=lax.rem(x + c + j, NX) * 2 + zh),
        )

    def n_own(j):
        return pltpu.make_async_copy(own_tile(own, r, j), near.at[pl.ds(j * B, B), :], n_local.at[j])

    def f_copy(j):
        return remote(
            near.at[pl.ds(j * B, B), :], far.at[pl.ds(j * B, B), :],
            f_send.at[j], f_recv.at[j], z_peer,
        )

    for j in range(SH):
        for d in (1, 3, 2):
            y_arrival(j, d).wait_recv()
            c_copy(j, d).start()
        for d in range(1, NY):

            @pl.when(lax.rem(c + NY - r, NY) == d)
            def _():
                c_arrival(j, d).wait_recv()

        @pl.when(lax.rem(c + j, NX) > 0)
        def _():
            n_copy(j).start()

        @pl.when(lax.rem(c + j, NX) == 0)
        def _():
            n_own(j).start()

    @pl.when(core == 1)
    def _():
        x_start(0)

    x_start(2)

    for j in range(SH):

        @pl.when(lax.rem(c + j, NX) > 0)
        def _():
            n_arrival(j).wait_recv()

        @pl.when(lax.rem(c + j, NX) == 0)
        def _():
            n_own(j).wait()

        f_copy(j).start()

    @pl.when(core == 1)
    def _():
        z_copy(2).start()

    for j in range(SH):
        for d in range(1, NY):

            @pl.when(lax.rem(c + NY - r, NY) != d)
            def _():
                c_arrival(j, d).wait_recv()

    @pl.loop(0, NY * SH)
    def _(t):
        value = own[rows_of(t), :]
        high = value.astype(jnp.bfloat16)
        own_hi[rows_of(t), :] = high
        own_lo[rows_of(t), :] = (value - high.astype(jnp.float32)).astype(jnp.bfloat16)

    def place(b, j):
        return 3 * (2 * lax.rem(x + c + j, NX) + (zh if b == 0 else 1 - zh)) + j

    def p_copy(b, j, d):
        n = (b * 3 + j) * 3 + d - 1
        return remote(
            product_out.at[pl.ds(n * B, B), :], product_ref.at[rows_of(place(b, j)), :],
            p_send.at[n], p_recv.at[n], y_peer(d),
        )

    def p_arrival(b, j, d):
        n = (b * 3 + j) * 3 + d - 1
        source = lax.rem(c + NY - d, NY)
        index = 3 * (2 * lax.rem(x + source + j, NX) + (zh if b == 0 else 1 - zh)) + j
        return remote(
            product_out.at[pl.ds(n * B, B), :], product_ref.at[rows_of(index), :],
            p_send.at[n], p_recv.at[n], y_peer(NY - d),
        )

    def p_own(b, j):
        n = 18 + b * 3 + j
        return pltpu.make_async_copy(
            product_out.at[pl.ds(n * B, B), :], product_ref.at[rows_of(place(b, j)), :],
            p_local.at[b * 3 + j],
        )

    for b in range(2):
        for j in range(SH):
            if b == 1:
                f_copy(j).wait_recv()
            value = (near, far)[b][j * B : (j + 1) * B, :]
            high = value.astype(jnp.bfloat16)
            low = (value - high.astype(jnp.float32)).astype(jnp.bfloat16)
            for d in (2, 1, 3, 0):
                col = lax.rem(c + d, NY)
                span = pl.ds(pl.multiple_of(col * WIDTH, WIDTH), WIDTH)
                got = (
                    times(high, own_lo[span, :]) + times(low, own_hi[span, :])
                    + times(high, own_hi[span, :])
                )
                n = 18 + b * 3 + j if d == 0 else (b * 3 + j) * 3 + d - 1
                product_out[n * B : (n + 1) * B, :] = got
                if d == 0:
                    p_own(b, j).start()
                else:
                    p_copy(b, j, d).start()

    panel_ref[...] = own[
        pl.ds(pl.multiple_of(c * WIDTH, WIDTH), WIDTH), pl.ds(pl.multiple_of(r * 256, 256), 256)
    ].T

    @pl.when(r > 0)
    def _():
        x_wait(0)

    def sum_copy(part):
        span = pl.ds(part * W, W)
        return pltpu.make_async_copy(out_part.at[span, :], sum_ref.at[span, :], sum_sem.at[part])

    def put_sum(i, j, value):
        span = (rows_of(i), slice(j * B, (j + 1) * B))
        out_part[span] = value + in_part[span]

    for part in range(3):
        z_copy(part).wait_send()
        if part > 0:
            z_copy(part).wait_recv()
            spread(part * WT, (part + 1) * WT, 0, put_sum)
        else:

            @pl.when(r == 0)
            def _():
                out_part[0:W, :] = in_part[0:W, :]

            @pl.when(r > 0)
            def _():
                z_copy(0).wait_recv()
                spread(0, WT, 0, put_sum)

        sum_copy(part).start()
        if part == 0:
            x_wait(2)

    for b in range(2):
        for j in range(SH):
            for d in range(1, NY):
                p_arrival(b, j, d).wait_recv()
            p_own(b, j).wait()
    for part in range(3):
        sum_copy(part).wait()

    for k in range(4):
        for d in range(1, NX):
            x_copy(k, d).wait_send()

    @pl.when(r > 0)
    def _():
        inverse_copy().wait_send()

    for j in range(SH):

        @pl.when(r == 0)
        def _():
            for d in range(1, 4):
                r_copy(j, d).wait_send()

        @pl.when(r > 1)
        def _():
            c_copy(j, 0).wait_send()

        for d in range(1, NY):
            y_copy(j, d).wait_send()
            c_copy(j, d).wait_send()

        @pl.when(lax.rem(c + j, NX) > 0)
        def _():
            n_copy(j).wait_send()

        f_copy(j).wait_send()
        for b in range(2):
            for d in range(1, NY):
                p_copy(b, j, d).wait_send()


def update_kernel(pattern_ref, sum_ref, product_ref, panel_in, front_ref, panel_ref):
    step = pl.program_id(0)
    r = lax.axis_index("row")
    panel_ref[...] = panel_in[...]
    for i in range(PB // STEPS):
        for j in range(SH):
            down = r * PB + step * (PB // STEPS) + i - WT
            right = lax.axis_index("col") * PB + lax.axis_index("grp") * SH + j - WT
            weight = pattern_ref[jnp.maximum(down, 0), jnp.maximum(right, 0)]
            weight = jnp.where((down >= 0) & (right >= 0), weight, 0).astype(jnp.float32)
            span = (slice(i * B, (i + 1) * B), slice(j * B, (j + 1) * B))
            front_ref[span] = sum_ref[span] - weight * product_ref[span]


def per_device(children, child_map, panel_inverse, pattern):
    anywhere = pl.BlockSpec(memory_space=pl.ANY)
    smem = pl.BlockSpec(memory_space=pltpu.SMEM)
    vmem = pl.BlockSpec(memory_space=pltpu.VMEM)
    f32, bf16 = jnp.float32, jnp.bfloat16
    dma = pltpu.SemaphoreType.DMA
    chunk = pltpu.VMEM((ZERO + 1, B, B), f32)
    sums, product, panel = pl.pallas_call(
        front_kernel,
        name="front",
        out_shape=(
            jax.ShapeDtypeStruct((BIG, WIDTH), f32),
            jax.ShapeDtypeStruct((BIG, WIDTH), f32),
            jax.ShapeDtypeStruct((256, WIDTH), f32),
        ),
        in_specs=[smem, anywhere, anywhere],
        out_specs=(anywhere, anywhere, vmem),
        scratch_shapes=[
            pltpu.SMEM((2 * NX * PB,), jnp.int32), pltpu.SMEM((2 * NX * 4,), jnp.int32),
            pltpu.VMEM((CB, HALF, B, B), f32), pltpu.VMEM((4, NX - 1, TILES, B, B), f32),
            chunk, chunk, chunk, chunk,
            pltpu.VMEM((BIG, WIDTH), f32), pltpu.VMEM((BIG, WIDTH), f32),
            pltpu.VMEM((24 * B, WIDTH), f32),
            pltpu.VMEM((NY * WIDTH, W), f32),
            pltpu.VMEM((NY * WIDTH, W), bf16), pltpu.VMEM((NY * WIDTH, W), bf16),
            pltpu.VMEM((WIDTH, W), f32), pltpu.VMEM((WIDTH, W), f32),
            pltpu.VMEM((W, W), f32),
            dma((2, CB)), dma((12,)), dma((12,)), dma((3,)), dma((3,)), dma(()), dma((3,)), dma(()),
            dma((9,)), dma((3,)), dma((12,)), dma((12,)), dma((9,)), dma((9,)),
            dma((3,)), dma((3,)), dma((3,)), dma((3,)), dma((3,)),
            dma((18,)), dma((18,)), dma((6,)), dma((3,)), pltpu.SemaphoreType.REGULAR,
        ],
        compiler_params=pltpu.CompilerParams(
            collective_id=1, has_side_effects=True, vmem_limit_bytes=63 * 2**20
        ),
    )(child_map, children.reshape(CB, B, CB * B), panel_inverse)
    block = pl.BlockSpec((BIG // STEPS, WIDTH), lambda i: (i, 0))
    part = pl.BlockSpec((256 // STEPS, WIDTH), lambda i: (i, 0))
    return pl.pallas_call(
        update_kernel,
        name="update",
        grid=(STEPS,),
        out_shape=(
            jax.ShapeDtypeStruct((BIG, WIDTH), f32),
            jax.ShapeDtypeStruct((256, WIDTH), f32),
        ),
        in_specs=[smem, block, block, part],
        out_specs=(block, part),
        compiler_params=pltpu.CompilerParams(vmem_limit_bytes=60 * 2**20),
    )(pattern, sums, product, panel)


def solution(mesh):
    placed = (P("grp", "row", "col"), P(), P("row", None), P())
    return jax.shard_map(
        per_device,
        mesh=mesh,
        in_specs=placed,
        out_specs=(P("row", ("grp", "col")), P("row", ("grp", "col"))),
        check_vma=False,
    )
```

```python
import jax
import jax.numpy as jnp
from jax import lax
from jax.experimental import pallas as pl
from jax.experimental.pallas import tpu as pltpu
from jax.sharding import PartitionSpec as P

MESH = pl.DeviceIdType.MESH
B = 128
GROUPS = 8
PB = 24
CB = 12
SH = 3
WT = 8
W = 1024
NX = 4
NY = 4
HALF = 6
HROWS = HALF * B
SLOTS = 2 * HROWS
TILES = 2 * HALF
ZERO = NX * 2 * HALF
NONE = 1000
WIDTH = SH * B
BIG = 3072
STEPS = 2


def front_kernel(
    map_ref, child_ref, inverse_ref,
    sum_ref, product_ref, panel_ref,
    rows_ref, cols_ref, held, staged,
    as_ref, ao_ref, bs_ref, bo_ref,
    out_part, in_part, product_out,
    own, own_hi, own_lo, near, far,
    inverse_all,
    held_sem, x_send, x_recv, z_send, z_recv, i_send, i_recv, i_local,
    r_send, r_recv, c_send, c_recv, y_send, y_recv, n_send, n_recv, n_local, f_send, f_recv,
    p_send, p_recv, p_local, sum_sem, go,
):
    g = lax.axis_index("grp")
    r = lax.axis_index("row")
    c = lax.axis_index("col")
    x, zh = g // 2, lax.rem(g, 2)

    def at(grp=None, row=None, col=None):
        return {
            "grp": g if grp is None else grp,
            "row": r if row is None else row,
            "col": c if col is None else col,
        }

    def x_peer(d):
        return at(grp=lax.rem(x + d, NX) * 2 + zh)

    def y_peer(d):
        return at(col=lax.rem(c + d, NY))

    z_peer = at(grp=2 * x + 1 - zh)

    def held_copy(h, q):
        return pltpu.make_async_copy(
            child_ref.at[pl.ds(h * HALF, HALF), :, pl.ds(q * B, B)], held.at[q], held_sem.at[h, q]
        )

    for q in range(CB):
        held_copy(0, q).start()
    core = lax.rem(r, 2)
    other_core = at(row=r + 1 - 2 * core)

    barrier = pltpu.get_barrier_semaphore()
    peers = [x_peer(d) for d in range(1, NX)] + [y_peer(d) for d in range(1, NY)]
    peers += [at(row=lax.rem(r + d, 4)) for d in range(1, 4)] + [z_peer]
    for peer in peers:
        pl.semaphore_signal(barrier, inc=1, device_id=peer, device_id_type=MESH)
    pl.semaphore_wait(barrier, len(peers))

    def remote(src, dst, send, recv, device):
        return pltpu.make_async_remote_copy(
            src_ref=src, dst_ref=dst, send_sem=send, recv_sem=recv,
            device_id=device, device_id_type=MESH,
        )

    chunks = [as_ref, ao_ref, bs_ref, bo_ref]

    def x_copy(k, d):
        return remote(
            staged.at[k, d - 1],
            chunks[k].at[pl.ds(x * TILES, TILES)],
            x_send.at[k * 3 + d - 1], x_recv.at[k * 3 + d - 1], x_peer(d),
        )

    def x_arrival(k, d):
        source = lax.rem(x + NX - d, NX)
        return remote(
            staged.at[k, d - 1],
            chunks[k].at[pl.ds(source * TILES, TILES)],
            x_send.at[k * 3 + d - 1], x_recv.at[k * 3 + d - 1], x_peer(NX - d),
        )

    def pack(k):
        places = []
        for d in range(NX):
            owner = lax.rem(x + d, NX) * 2 + (zh if k % 2 == 0 else 1 - zh)
            low = c * PB + owner * SH
            before = sum((map_ref[g, c * CB + q] < low).astype(jnp.int32) for q in range(CB))
            for slot in range(2):
                places.append((d, slot, jnp.minimum(before + slot, CB - 1)))

        @pl.loop(0, HALF)
        def _(a):
            for d, slot, q in places:
                if d == 0:
                    chunks[k][x * TILES + slot * HALF + a] = held[q, a]
                else:
                    staged[k, d - 1, slot * HALF + a] = held[q, a]

    def x_start(k):
        for d in (2, 1, 3):
            x_copy(k, d).start()

    def x_wait(k):
        for d in range(1, NX):
            x_arrival(k, d).wait_recv()

    def inverse_copy():
        return remote(
            inverse_ref,
            inverse_all.at[pl.ds(pl.multiple_of(r * 256, 256), 256), :],
            i_send, i_recv.at[r - 1], at(row=0),
        )

    for ref in chunks:
        ref[ZERO] = jnp.zeros((B, B), jnp.float32)

    @pl.when(r == 0)
    def _():
        pltpu.make_async_copy(inverse_ref, inverse_all.at[pl.ds(0, 256), :], i_local).start()

    for q in range(CB):
        held_copy(0, q).wait()
    pack(1)

    @pl.when(core == 0)
    def _():
        x_start(1)

    pack(0)

    @pl.when(r == 0)
    def _():
        x_start(0)

    for q in range(CB):
        held_copy(1, q).start()

    @pl.when(r > 0)
    def _():
        inverse_copy().start()

    for n in range(NX):
        child = 2 * n + zh

        def place_row(i, at_tile):
            found = map_ref[child, r * CB + jnp.minimum(at_tile, CB - 1)] == r * PB + i
            hit = found & (at_tile < CB)
            rows_ref[n * PB + i] = jnp.where(hit & (at_tile < HALF), at_tile, NONE)
            rows_ref[(NX + n) * PB + i] = jnp.where(hit & (at_tile >= HALF), at_tile - HALF, NONE)
            return at_tile + hit.astype(jnp.int32)

        lax.fori_loop(0, PB, place_row, jnp.int32(0))
        for d in range(2):
            low = c * PB + (2 * x + (zh if d == 0 else 1 - zh)) * SH
            slot = jnp.int32(0)
            for j in range(SH):
                hit = sum(
                    (map_ref[child, c * CB + q] == low + j).astype(jnp.int32) for q in range(CB)
                )
                cols_ref[(d * NX + n) * 4 + j] = jnp.where(hit > 0, (n * 2 + slot) * HALF, NONE)
                slot = slot + hit

    for q in range(CB):
        held_copy(1, q).wait()
    pack(3)
    pack(2)

    def tile(d, i, j, use):
        total = None
        for s in range(NX):
            for h, ref in use:
                index = jnp.minimum(
                    rows_ref[h * NX * PB + s * PB + i] + cols_ref[d * NX * 4 + s * 4 + j], ZERO
                )
                value = ref[index]
                total = value if total is None else total + value
        return total

    def spread(first, last, d, put):
        a_ref, b_ref = (as_ref, bs_ref) if d == 0 else (ao_ref, bo_ref)
        for low, high, use in (
            (0, 9, ((0, a_ref),)),
            (9, 15, ((0, a_ref), (1, b_ref))),
            (15, 24, ((1, b_ref),)),
        ):
            low, high = max(low, first), min(high, last)
            if low < high:

                @pl.loop(low, high)
                def _(i):
                    for j in range(SH):
                        put(i, j, tile(d, i, j, use))

    def rows_of(i):
        return pl.ds(pl.multiple_of(i * B, B), B)

    def put_out(i, j, value):
        out_part[rows_of(i), j * B : (j + 1) * B] = value

    def z_copy(part):
        span = pl.ds(part * W, W)
        return remote(
            out_part.at[span, :], in_part.at[span, :],
            z_send.at[part], z_recv.at[part], z_peer,
        )

    def own_tile(ref, col, j):
        return ref.at[pl.ds(pl.multiple_of(col * WIDTH + j * B, B), B), :]

    def own_half(col, j, k):
        start = col * WIDTH + j * B + k * (B // 2)
        return own.at[pl.ds(pl.multiple_of(start, B // 2), B // 2), :]

    def r_copy(j, d):
        part = own_tile(own, c, j) if d == 1 else own_half(c, j, d - 2)
        return remote(part, part, r_send.at[(d - 1) * 3 + j], r_recv.at[j], at(row=d))

    def c_copy(j, d):
        part = own_half(lax.rem(c + NY - d, NY), j, core)
        return remote(part, part, c_send.at[d * 3 + j], c_recv.at[d * 3 + j], other_core)

    def c_arrival(j, d):
        part = own_half(lax.rem(c + NY - d, NY), j, 1 - core)
        return remote(part, part, c_send.at[d * 3 + j], c_recv.at[d * 3 + j], other_core)

    def y_copy(j, d):
        part = own_half(c, j, core)
        n = (d - 1) * 3 + j
        return remote(part, part, y_send.at[n], y_recv.at[n], y_peer(d))

    def y_arrival(j, d):
        part = own_half(lax.rem(c + NY - d, NY), j, core)
        n = (d - 1) * 3 + j
        return remote(part, part, y_send.at[n], y_recv.at[n], y_peer(NY - d))

    def times(a, b):
        return lax.dot_general(a, b, (((1,), (1,)), ((), ())), preferred_element_type=jnp.float32)

    @pl.when(r == 0)
    def _():
        x_wait(1)
        spread(0, WT, 1, put_out)
        z_copy(0).start()
        for k in range(1, 4):
            remote(
                inverse_ref, inverse_all.at[pl.ds(k * 256, 256), :],
                i_send, i_recv.at[k - 1], at(row=k),
            ).wait_recv()
        pltpu.make_async_copy(inverse_ref, inverse_all.at[pl.ds(0, 256), :], i_local).wait()

        @pl.loop(0, WT)
        def _(i):
            value = inverse_all[rows_of(i), :]
            high = value.astype(jnp.bfloat16)
            own_hi[rows_of(i), :] = high
            own_lo[rows_of(i), :] = (value - high.astype(jnp.float32)).astype(jnp.bfloat16)

        x_wait(0)
        x_start(3)

        z_copy(0).wait_recv()

        def put_top(i, j, value):
            span = (rows_of(i), slice(j * B, (j + 1) * B))
            in_part[span] = in_part[span] + value

        spread(0, WT, 0, put_top)
        top = slice(W, W + WIDTH)
        for i in range(WT):
            value = in_part[i * B : (i + 1) * B, :].T
            high = value.astype(jnp.bfloat16)
            own_hi[top, i * B : (i + 1) * B] = high
            own_lo[top, i * B : (i + 1) * B] = (value - high.astype(jnp.float32)).astype(jnp.bfloat16)
        for j in range(SH):
            piece = slice(W + j * B, W + (j + 1) * B)
            rows = pl.ds(pl.multiple_of(c * WIDTH + j * B, B), B)
            for k in range(4):
                part = slice(k * 256, (k + 1) * 256)
                own[rows, part] = (
                    times(own_hi[piece, :], own_lo[part, :])
                    + times(own_lo[piece, :], own_hi[part, :])
                    + times(own_hi[piece, :], own_hi[part, :])
                )
            r_copy(j, 2).start()
            r_copy(j, 3).start()
            r_copy(j, 1).start()
            for d in range(1, NY):
                y_copy(j, d).start()
        x_wait(3)
        pl.semaphore_signal(go, inc=1, device_id=other_core, device_id_type=MESH)

    def take(d):
        for j in range(SH):
            part = own_tile(own, c, j) if d == 1 else own_half(c, j, core)
            remote(part, part, r_send.at[j], r_recv.at[j], at(row=0)).wait_recv()
            for d2 in range(1, NY):
                y_copy(j, d2).start()
            if d > 1:
                c_copy(j, 0).start()

    @pl.when(core == 1)
    def _():
        pl.semaphore_wait(go, 1)
        x_start(1)
        x_start(3)

    @pl.when(r == 2)
    def _():
        x_wait(1)
        pl.semaphore_signal(go, inc=1, device_id=other_core, device_id_type=MESH)
        x_start(3)
        spread(0, WT, 1, put_out)
        z_copy(0).start()
        x_wait(3)
        x_start(0)

    @pl.when(r == 1)
    def _():
        take(1)

    @pl.when(core == 1)
    def _():
        x_wait(1)
        spread(0, WT, 1, put_out)
        z_copy(0).start()

    @pl.when(r == 3)
    def _():
        take(3)

    @pl.when(core == 1)
    def _():
        x_wait(3)

    spread(WT, PB, 1, put_out)

    z_copy(1).start()

    @pl.when(core == 0)
    def _():
        z_copy(2).start()

    @pl.when(r == 2)
    def _():
        take(2)

    @pl.when(r > 1)
    def _():
        for j in range(SH):
            c_arrival(j, 0).wait_recv()

    def n_copy(j):
        return remote(
            own_tile(own, r, j), near.at[pl.ds(j * B, B), :],
            n_send.at[j], n_recv.at[j], at(grp=lax.rem(x + 2 * NX - c - j, NX) * 2 + zh),
        )

    def n_arrival(j):
        return remote(
            own_tile(own, r, j), near.at[pl.ds(j * B, B), :],
            n_send.at[j], n_recv.at[j], at(grp=lax.rem(x + c + j, NX) * 2 + zh),
        )

    def n_own(j):
        return pltpu.make_async_copy(own_tile(own, r, j), near.at[pl.ds(j * B, B), :], n_local.at[j])

    def f_copy(j):
        return remote(
            near.at[pl.ds(j * B, B), :], far.at[pl.ds(j * B, B), :],
            f_send.at[j], f_recv.at[j], z_peer,
        )

    for j in range(SH):
        for d in (1, 3, 2):
            y_arrival(j, d).wait_recv()
            c_copy(j, d).start()
        for d in range(1, NY):

            @pl.when(lax.rem(c + NY - r, NY) == d)
            def _():
                c_arrival(j, d).wait_recv()

        @pl.when(lax.rem(c + j, NX) > 0)
        def _():
            n_copy(j).start()

        @pl.when(lax.rem(c + j, NX) == 0)
        def _():
            n_own(j).start()

    @pl.when(core == 1)
    def _():
        x_start(0)

    x_start(2)

    for j in range(SH):

        @pl.when(lax.rem(c + j, NX) > 0)
        def _():
            n_arrival(j).wait_recv()

        @pl.when(lax.rem(c + j, NX) == 0)
        def _():
            n_own(j).wait()

        f_copy(j).start()

    @pl.when(core == 1)
    def _():
        z_copy(2).start()

    for j in range(SH):
        for d in range(1, NY):

            @pl.when(lax.rem(c + NY - r, NY) != d)
            def _():
                c_arrival(j, d).wait_recv()

    @pl.loop(0, NY * SH)
    def _(t):
        value = own[rows_of(t), :]
        high = value.astype(jnp.bfloat16)
        own_hi[rows_of(t), :] = high
        own_lo[rows_of(t), :] = (value - high.astype(jnp.float32)).astype(jnp.bfloat16)

    def place(b, j):
        return 3 * (2 * lax.rem(x + c + j, NX) + (zh if b == 0 else 1 - zh)) + j

    def p_copy(b, j, d):
        n = (b * 3 + j) * 3 + d - 1
        return remote(
            product_out.at[pl.ds(n * B, B), :], product_ref.at[rows_of(place(b, j)), :],
            p_send.at[n], p_recv.at[n], y_peer(d),
        )

    def p_arrival(b, j, d):
        n = (b * 3 + j) * 3 + d - 1
        source = lax.rem(c + NY - d, NY)
        index = 3 * (2 * lax.rem(x + source + j, NX) + (zh if b == 0 else 1 - zh)) + j
        return remote(
            product_out.at[pl.ds(n * B, B), :], product_ref.at[rows_of(index), :],
            p_send.at[n], p_recv.at[n], y_peer(NY - d),
        )

    def p_own(b, j):
        n = 18 + b * 3 + j
        return pltpu.make_async_copy(
            product_out.at[pl.ds(n * B, B), :], product_ref.at[rows_of(place(b, j)), :],
            p_local.at[b * 3 + j],
        )

    for b in range(2):
        for j in range(SH):
            if b == 1:
                f_copy(j).wait_recv()
            value = (near, far)[b][j * B : (j + 1) * B, :]
            high = value.astype(jnp.bfloat16)
            low = (value - high.astype(jnp.float32)).astype(jnp.bfloat16)
            for d in (2, 1, 3, 0):
                col = lax.rem(c + d, NY)
                span = pl.ds(pl.multiple_of(col * WIDTH, WIDTH), WIDTH)
                got = (
                    times(high, own_lo[span, :]) + times(low, own_hi[span, :])
                    + times(high, own_hi[span, :])
                )
                n = 18 + b * 3 + j if d == 0 else (b * 3 + j) * 3 + d - 1
                product_out[n * B : (n + 1) * B, :] = got
                if d == 0:
                    p_own(b, j).start()
                else:
                    p_copy(b, j, d).start()

    panel_ref[...] = own[
        pl.ds(pl.multiple_of(c * WIDTH, WIDTH), WIDTH), pl.ds(pl.multiple_of(r * 256, 256), 256)
    ].T

    @pl.when(r > 0)
    def _():
        x_wait(0)

    def sum_copy(part):
        span = pl.ds(part * W, W)
        return pltpu.make_async_copy(out_part.at[span, :], sum_ref.at[span, :], sum_sem.at[part])

    def put_sum(i, j, value):
        span = (rows_of(i), slice(j * B, (j + 1) * B))
        out_part[span] = value + in_part[span]

    for part in range(3):
        z_copy(part).wait_send()
        if part > 0:
            z_copy(part).wait_recv()
            spread(part * WT, (part + 1) * WT, 0, put_sum)
        else:

            @pl.when(r == 0)
            def _():
                out_part[0:W, :] = in_part[0:W, :]

            @pl.when(r > 0)
            def _():
                z_copy(0).wait_recv()
                spread(0, WT, 0, put_sum)

        sum_copy(part).start()
        if part == 0:
            x_wait(2)

    for b in range(2):
        for j in range(SH):
            for d in range(1, NY):
                p_arrival(b, j, d).wait_recv()
            p_own(b, j).wait()
    for part in range(3):
        sum_copy(part).wait()

    for k in range(4):
        for d in range(1, NX):
            x_copy(k, d).wait_send()

    @pl.when(r > 0)
    def _():
        inverse_copy().wait_send()

    for j in range(SH):

        @pl.when(r == 0)
        def _():
            for d in range(1, 4):
                r_copy(j, d).wait_send()

        @pl.when(r > 1)
        def _():
            c_copy(j, 0).wait_send()

        for d in range(1, NY):
            y_copy(j, d).wait_send()
            c_copy(j, d).wait_send()

        @pl.when(lax.rem(c + j, NX) > 0)
        def _():
            n_copy(j).wait_send()

        f_copy(j).wait_send()
        for b in range(2):
            for d in range(1, NY):
                p_copy(b, j, d).wait_send()


def update_kernel(pattern_ref, sum_ref, product_ref, panel_in, front_ref, panel_ref):
    step = pl.program_id(0)
    r = lax.axis_index("row")
    panel_ref[...] = panel_in[...]
    for i in range(PB // STEPS):
        for j in range(SH):
            down = r * PB + step * (PB // STEPS) + i - WT
            right = lax.axis_index("col") * PB + lax.axis_index("grp") * SH + j - WT
            weight = pattern_ref[jnp.maximum(down, 0), jnp.maximum(right, 0)]
            weight = jnp.where((down >= 0) & (right >= 0), weight, 0).astype(jnp.float32)
            span = (slice(i * B, (i + 1) * B), slice(j * B, (j + 1) * B))
            front_ref[span] = sum_ref[span] - weight * product_ref[span]


def per_device(children, child_map, panel_inverse, pattern):
    anywhere = pl.BlockSpec(memory_space=pl.ANY)
    smem = pl.BlockSpec(memory_space=pltpu.SMEM)
    vmem = pl.BlockSpec(memory_space=pltpu.VMEM)
    f32, bf16 = jnp.float32, jnp.bfloat16
    dma = pltpu.SemaphoreType.DMA
    chunk = pltpu.VMEM((ZERO + 1, B, B), f32)
    sums, product, panel = pl.pallas_call(
        front_kernel,
        name="front",
        out_shape=(
            jax.ShapeDtypeStruct((BIG, WIDTH), f32),
            jax.ShapeDtypeStruct((BIG, WIDTH), f32),
            jax.ShapeDtypeStruct((256, WIDTH), f32),
        ),
        in_specs=[smem, anywhere, anywhere],
        out_specs=(anywhere, anywhere, vmem),
        scratch_shapes=[
            pltpu.SMEM((2 * NX * PB,), jnp.int32), pltpu.SMEM((2 * NX * 4,), jnp.int32),
            pltpu.VMEM((CB, HALF, B, B), f32), pltpu.VMEM((4, NX - 1, TILES, B, B), f32),
            chunk, chunk, chunk, chunk,
            pltpu.VMEM((BIG, WIDTH), f32), pltpu.VMEM((BIG, WIDTH), f32),
            pltpu.VMEM((24 * B, WIDTH), f32),
            pltpu.VMEM((NY * WIDTH, W), f32),
            pltpu.VMEM((NY * WIDTH, W), bf16), pltpu.VMEM((NY * WIDTH, W), bf16),
            pltpu.VMEM((WIDTH, W), f32), pltpu.VMEM((WIDTH, W), f32),
            pltpu.VMEM((W, W), f32),
            dma((2, CB)), dma((12,)), dma((12,)), dma((3,)), dma((3,)), dma(()), dma((3,)), dma(()),
            dma((9,)), dma((3,)), dma((12,)), dma((12,)), dma((9,)), dma((9,)),
            dma((3,)), dma((3,)), dma((3,)), dma((3,)), dma((3,)),
            dma((18,)), dma((18,)), dma((6,)), dma((3,)), pltpu.SemaphoreType.REGULAR,
        ],
        compiler_params=pltpu.CompilerParams(
            collective_id=1, has_side_effects=True, vmem_limit_bytes=63 * 2**20
        ),
    )(child_map, children.reshape(CB, B, CB * B), panel_inverse)
    block = pl.BlockSpec((BIG // STEPS, WIDTH), lambda i: (i, 0))
    part = pl.BlockSpec((256 // STEPS, WIDTH), lambda i: (i, 0))
    return pl.pallas_call(
        update_kernel,
        name="update",
        grid=(STEPS,),
        out_shape=(
            jax.ShapeDtypeStruct((BIG, WIDTH), f32),
            jax.ShapeDtypeStruct((256, WIDTH), f32),
        ),
        in_specs=[smem, block, block, part],
        out_specs=(block, part),
        compiler_params=pltpu.CompilerParams(vmem_limit_bytes=60 * 2**20),
    )(pattern, sums, product, panel)


def solution(mesh):
    placed = (P("grp", "row", "col"), P(), P("row", None), P())
    return jax.shard_map(
        per_device,
        mesh=mesh,
        in_specs=placed,
        out_specs=(P("row", ("grp", "col")), P("row", ("grp", "col"))),
        check_vma=False,
    )
```
